32 devices in a mesh: dp: 8 (over y, x, core), tensor: 4 (over z).
Axes of the slice: x: 2, y: 2, z: 4, core: 2. Of those that a mesh axis runs over, the one named last changes fastest.
Arguments:
- tokens: bfloat16 [32768, 768], P(('dp', 'tensor')), may hold values from -6 to 6
- ln_gains: bfloat16 [2, 768], P(None, ('dp', 'tensor')), may hold values from 0.5 to 1.5
- ln_biases: bfloat16 [2, 768], P(None, ('dp', 'tensor')), may hold values from -4 to 4
- w_query: bfloat16 [768, 768], P('dp', 'tensor'), may hold values from -0.21875 to 0.21875
- w_key: bfloat16 [768, 768], P('dp', 'tensor'), may hold values from -0.21875 to 0.21875
- w_value: bfloat16 [768, 768], P('dp', 'tensor'), may hold values from -0.21875 to 0.21875
- query_bias: bfloat16 [768], P('tensor'), may hold values from -4 to 4
- key_bias: bfloat16 [768], P('tensor'), may hold values from -4 to 4
- value_bias: bfloat16 [768], P('tensor'), may hold values from -1.5 to 1.5
- w_output: bfloat16 [768, 768], P('tensor', 'dp'), may hold values from -1.25 to 1.25
- w_up: bfloat16 [768, 3072], P('dp', 'tensor'), may hold values from -0.21875 to 0.21875
- up_bias: bfloat16 [3072], P('tensor'), may hold values from -4 to 4
- w_down: bfloat16 [3072, 768], P('tensor', 'dp'), may hold values from -0.109375 to 0.109375
- out_biases: bfloat16 [2, 768], P(None, ('dp', 'tensor')), may hold values from -4 to 4
- cotangent: bfloat16 [32768, 768], P(('dp', 'tensor')), may hold values from -6 to 6
Outputs:
- block_out: bfloat16 [32768, 768], P(('dp', 'tensor'))
- grad_tokens: float32 [32768, 768], P(('dp', 'tensor'))
- grad_ln_gains: float32 [2, 768], P(None, ('dp', 'tensor'))
- grad_ln_biases: float32 [2, 768], P(None, ('dp', 'tensor'))
- grad_w_query: float32 [768, 768], P('dp', 'tensor')
- grad_w_key: float32 [768, 768], P('dp', 'tensor')
- grad_w_value: float32 [768, 768], P('dp', 'tensor')
- grad_query_bias: float32 [768], P('tensor')
- grad_key_bias: float32 [768], P('tensor')
- grad_value_bias: float32 [768], P('tensor')
- grad_w_output: float32 [768, 768], P('tensor', 'dp')
- grad_w_up: float32 [768, 3072], P('dp', 'tensor')
- grad_up_bias: float32 [3072], P('tensor')
- grad_w_down: float32 [3072, 768], P('tensor', 'dp')
- grad_out_biases: float32 [2, 768], P(None, ('dp', 'tensor'))
The draws below stay inside these ranges and needn't reach their ends.
All inputs are finite; a program needn't handle non-finite values.
Results may differ from the reference program's by a relative error of at most 0.012.
The reference program's roundings to bfloat16 on the way count: a program that leaves them out, or rounds other values in their place, can miss the bound.
Values may be sent and summed in bfloat16 or wider, within the bound.
No kernel may reach another device: no remote copies, remote signals or barrier semaphores. Data moves between devices by JAX's collectives and lax.ppermute only.
A program may use at most 192 MiB of HBM per device.

```python
import jax
import jax.numpy as jnp
from jax import lax

D = 768
HEADS = 12
HEAD_DIM = 64
ROT = 16
FF = 3072
SEQ_LEN = 1024
TOKENS = 32768


def block_levels(key, extent, cuts, least, top_value):
    loudness, own = 1.0, jax.random.fold_in(key, 6)
    for position, parts in cuts:
        steps = jnp.exp(jax.random.uniform(jax.random.fold_in(own, position), (parts,), jnp.float32, least / len(cuts), top_value / len(cuts)))
        loudness = loudness * jnp.repeat(steps, extent[position] // parts).reshape([-1 if axis == position else 1 for axis in range(len(extent))])
    return loudness


def gaussian(key, extent, width, limit, split=(), held_as=jnp.bfloat16):
    entries = width * jax.random.normal(key, extent, jnp.float32)
    if split:
        entries = entries * block_levels(key, extent, split, -0.22, 0.18)
    return jnp.clip(entries, -limit, limit).astype(held_as)


def setup_inputs(seed: int = 0) -> dict:
    key_of = jax.random.split(jax.random.key(seed), 16)
    tokens = gaussian(key_of[0], (TOKENS, D), 1.0, 6.0, ((0, 32),))
    ln_gains = jnp.clip(1.0 + 0.1 * jax.random.normal(key_of[1], (2, D), jnp.float32), 0.5, 1.5).astype(jnp.bfloat16)
    ln_biases = gaussian(key_of[2], (2, D), 0.3, 4.0, ((1, 32),))
    w_query = gaussian(key_of[3], (D, D), D ** -0.5, 0.21875, ((0, 8), (1, 4)))
    w_key = gaussian(key_of[4], (D, D), D ** -0.5, 0.21875, ((0, 8), (1, 4)))
    w_value = gaussian(key_of[5], (D, D), D ** -0.5, 0.21875, ((0, 8), (1, 4)))
    query_bias = gaussian(key_of[6], (D,), 0.3, 4.0, ((0, 4),))
    key_bias = gaussian(key_of[7], (D,), 0.3, 4.0, ((0, 4),))
    value_bias = gaussian(key_of[8], (D,), 0.1, 1.5, ((0, 4),))
    w_output = gaussian(key_of[9], (D, D), (D // 32) ** -0.5, 1.25, ((0, 4), (1, 8)))
    w_up = gaussian(key_of[10], (D, FF), D ** -0.5, 0.21875, ((0, 8), (1, 4)))
    up_bias = gaussian(key_of[11], (FF,), 0.3, 4.0, ((0, 4),))
    w_down = gaussian(key_of[12], (FF, D), FF ** -0.5, 0.109375, ((0, 4), (1, 8)))
    out_biases = gaussian(key_of[13], (2, D), 0.3, 4.0, ((1, 32),))
    cotangent = gaussian(key_of[14], (TOKENS, D), 1.0, 6.0, ((0, 32),))
    return dict(tokens=tokens, ln_gains=ln_gains, ln_biases=ln_biases, w_query=w_query, w_key=w_key, w_value=w_value, query_bias=query_bias, key_bias=key_bias, value_bias=value_bias, w_output=w_output, w_up=w_up, up_bias=up_bias, w_down=w_down, out_biases=out_biases, cotangent=cotangent)


EPSILON = 1e-05
HIGH = lax.Precision.HIGHEST

@jax.custom_vjp
def low(v):
    return lax.optimization_barrier(v.astype(jnp.bfloat16)).astype(jnp.float32)

@jax.custom_vjp
def low_back(v):
    return v

def low_keep(v):
    return (low(v), None)

def low_pass(kept, grad):
    return (grad,)

def back_keep(v):
    return (v, None)

def back_low(kept, grad):
    return (low(grad),)
low.defvjp(low_keep, low_pass)
low_back.defvjp(back_keep, back_low)

def matmul(left_side, right_side):
    return jnp.dot(left_side, right_side, precision=HIGH, preferred_element_type=jnp.float32)

def layer_norm(rows_in, gain_row, bias_row):
    center = rows_in - lax.optimization_barrier(jnp.mean(rows_in, axis=1, keepdims=True))
    normed = center * lax.rsqrt(lax.optimization_barrier(jnp.mean(center * center, axis=1, keepdims=True)) + EPSILON)
    return normed * gain_row + bias_row

def gelu_exact(values):
    return jax.nn.gelu(values, approximate=False)

def angle_tables():
    positions = jnp.arange(SEQ_LEN, dtype=jnp.float32)
    frequency = 10000.0 ** (-2.0 * jnp.arange(ROT // 2, dtype=jnp.float32) / ROT)
    angles = positions[:, None] * frequency[None, :]
    return (jnp.cos(angles)[:, None, :], jnp.sin(angles)[:, None, :])

def rotate(values, cosine, sine_part, direction_sign):
    half_rot = ROT // 2
    first_part = values[..., :half_rot]
    second = values[..., half_rot:ROT]
    return jnp.concatenate([first_part * cosine - direction_sign * second * sine_part, second * cosine + direction_sign * first_part * sine_part, values[..., ROT:]], axis=-1)

def attend(pieces):
    queries, key_rows, value_rows = pieces
    scores = low_back(jnp.einsum('qhd,khd->hqk', queries, key_rows, precision=HIGH))
    allowed = lax.broadcasted_iota(jnp.int32, (SEQ_LEN, SEQ_LEN), 0) >= lax.broadcasted_iota(jnp.int32, (SEQ_LEN, SEQ_LEN), 1)
    scores = jnp.where(allowed[None], scores, -1e+30)
    row_top = lax.optimization_barrier(jnp.max(scores, axis=2, keepdims=True))
    exp_rows = jnp.exp(scores - row_top)
    prob_rows = exp_rows / lax.optimization_barrier(jnp.sum(exp_rows, axis=2, keepdims=True))
    return jnp.einsum('hqk,khd->qhd', low(prob_rows), value_rows, precision=HIGH)

def forward(rows_in, gain_rows, norm_bias, w_query, w_key, w_value, query_bias, key_bias, value_bias, w_output, w_up, up_bias, w_down, branch_bias):
    attn_in = low(layer_norm(rows_in, gain_rows[0], norm_bias[0]))
    mlp_in = low(layer_norm(rows_in, gain_rows[1], norm_bias[1]))
    head_shape = (-1, SEQ_LEN, HEADS, HEAD_DIM)
    cosine, sine_part = angle_tables()
    query_pre = low_back(matmul(attn_in, w_query) + query_bias).reshape(head_shape)
    key_pre = low_back(matmul(attn_in, w_key) + key_bias).reshape(head_shape)
    value_rows = low_back(low(matmul(attn_in, w_value) + value_bias)).reshape(head_shape)
    query_rot = low(rotate(query_pre, cosine, sine_part, 1.0) * HEAD_DIM ** (-0.5))
    key_rot = low(rotate(key_pre, cosine, sine_part, 1.0))
    attn_out = lax.map(jax.checkpoint(attend), (query_rot, key_rot, value_rows))
    attn_flat = low_back(low(attn_out.reshape(-1, D)))
    up_pre = low_back(matmul(mlp_in, w_up) + up_bias)
    up_act = low(gelu_exact(up_pre))
    return rows_in + matmul(attn_flat, w_output) + branch_bias[0] + matmul(up_act, w_down) + branch_bias[1]

def reference(tokens, ln_gains, ln_biases, w_query, w_key, w_value, query_bias, key_bias, value_bias, w_output, w_up, up_bias, w_down, out_biases, cotangent):
    block_out, pullback = jax.vjp(forward, tokens.astype(jnp.float32), ln_gains.astype(jnp.float32), ln_biases.astype(jnp.float32), w_query.astype(jnp.float32), w_key.astype(jnp.float32), w_value.astype(jnp.float32), query_bias.astype(jnp.float32), key_bias.astype(jnp.float32), value_bias.astype(jnp.float32), w_output.astype(jnp.float32), w_up.astype(jnp.float32), up_bias.astype(jnp.float32), w_down.astype(jnp.float32), out_biases.astype(jnp.float32))
    grads = pullback(cotangent.astype(jnp.float32))
    return (block_out.astype(jnp.bfloat16), grads[0], grads[1], grads[2], grads[3], grads[4], grads[5], grads[6], grads[7], grads[8], grads[9], grads[10], grads[11], grads[12], grads[13])
```

```python
import functools

import jax
import jax.numpy as jnp
from jax import lax
from jax.experimental import pallas as pl
from jax.experimental.pallas import tpu as pltpu
from jax.sharding import PartitionSpec as P

HEAD_DIM = 64
ROT = 16
SEQ_LEN = 1024
EPSILON = 1e-05
PAIR = 2 * HEAD_DIM
Q_ROWS = 256
M_ROWS = 512
N_ROWS = 256
FF_CHUNK = 256
VMEM = 60 * 1024 * 1024
F32 = jnp.float32
BF16 = jnp.bfloat16


def dot_nn(a, b):
    return jnp.dot(a, b, preferred_element_type=F32)


def dot_nt(a, b):
    return lax.dot_general(a, b, (((1,), (1,)), ((), ())), preferred_element_type=F32)


def dot_tn(a, b):
    return lax.dot_general(a, b, (((0,), (0,)), ((), ())), preferred_element_type=F32)


def layer_stats(rows):
    center = rows - jnp.mean(rows, axis=1, keepdims=True)
    inverse = lax.rsqrt(jnp.mean(center * center, axis=1, keepdims=True) + EPSILON)
    return center * inverse, inverse


def norm_kernel(x_ref, dy_ref, gain_ref, bias_ref, a_ref, m_ref, at_ref, mt_ref, dyt_ref, sum_ref):
    normed, _ = layer_stats(x_ref[...].astype(F32))
    a = normed * gain_ref[0:1] + bias_ref[0:1]
    m = normed * gain_ref[1:2] + bias_ref[1:2]
    dy = dy_ref[...].astype(F32)
    a_ref[...] = a.astype(BF16)
    m_ref[...] = m.astype(BF16)
    at_ref[...] = a.T.astype(BF16)
    mt_ref[...] = m.T.astype(BF16)
    dyt_ref[...] = dy.T.astype(BF16)

    @pl.when(pl.program_id(0) == 0)
    def _():
        sum_ref[...] = jnp.zeros_like(sum_ref)

    sum_ref[...] += jnp.sum(dy, axis=0, keepdims=True)


def rope_mix(u, tables, sign):
    c, s1, s2 = tables
    turned = pltpu.roll(u, PAIR - ROT // 2, 1) * s1 + pltpu.roll(u, ROT // 2, 1) * s2
    return u * c + turned if sign > 0 else u * c - turned


def attn_kernel(
    heads,
    x_ref,
    xt_ref,
    dy_ref,
    dyt_ref,
    w_ref,
    bqk_ref,
    bv_ref,
    c_ref,
    s1_ref,
    s2_ref,
    y_ref,
    dx_ref,
    gw_ref,
    dbqk_ref,
    dbv_ref,
    qk_s,
    v_s,
    do_s,
    dqk_s,
    dv_s,
    o_s,
    dq_s,
    dkt_s,
    dvt_s,
    oacc_s,
):
    nqk = heads * PAIR
    nv = heads * HEAD_DIM
    wqk = w_ref[:, :nqk]
    wv = w_ref[:, nqk : nqk + nv]
    wo = w_ref[:, nqk + nv :]
    qk = dot_nn(x_ref[...], wqk) + bqk_ref[...]
    for t in range(heads):
        u = qk[:, t * PAIR : (t + 1) * PAIR]
        qk_s[t] = rope_mix(u, (c_ref[...], s1_ref[...], s2_ref[...]), 1).astype(BF16)
    v = (dot_nn(x_ref[...], wv) + bv_ref[...]).astype(BF16)
    do = dot_nn(dy_ref[...], wo).astype(BF16)
    for p in range(heads // 2):
        v_s[p] = v[:, p * PAIR : (p + 1) * PAIR]
        do_s[p] = do[:, p * PAIR : (p + 1) * PAIR]

    lane = lax.broadcasted_iota(jnp.int32, (1, PAIR), 1)
    low = lane < HEAD_DIM
    below = lax.broadcasted_iota(jnp.int32, (Q_ROWS, Q_ROWS), 0) >= lax.broadcasted_iota(
        jnp.int32, (Q_ROWS, Q_ROWS), 1
    )

    def one_head(t, carry):
        p = t // 2
        odd = t % 2
        mine = (lane // HEAD_DIM) == odd
        qk_h = qk_s[t]
        kq = pltpu.roll(qk_h.astype(F32), HEAD_DIM, 1).astype(BF16)
        q_only = jnp.where(low, qk_h, jnp.zeros_like(qk_h))
        v_h = v_s[p]
        v_h = jnp.where(mine, v_h, jnp.zeros_like(v_h))
        do_h = do_s[p]
        do_h = jnp.where(mine, do_h, jnp.zeros_like(do_h))

        @pl.when(odd == 0)
        def _():
            dvt_s[...] = jnp.zeros_like(dvt_s)
            oacc_s[...] = jnp.zeros_like(oacc_s)

        blocks = SEQ_LEN // Q_ROWS
        for step, i in enumerate(reversed(range(blocks))):
            r = slice(i * Q_ROWS, (i + 1) * Q_ROWS)
            n = (i + 1) * Q_ROWS
            s = dot_nt(q_only[r], kq[:n])
            tail = jnp.where(below, s[:, n - Q_ROWS :], -1e30)
            s = tail if i == 0 else jnp.concatenate([s[:, : n - Q_ROWS], tail], axis=1)
            top = jnp.max(s, axis=1, keepdims=True)
            e = jnp.exp(s - top)
            total = jnp.sum(e, axis=1, keepdims=True)
            prob = e * (1.0 / total)
            prob_low = prob.astype(BF16)
            oacc_s[r, :] += dot_nn(prob_low, v_h[:n])
            dp = dot_nt(do_h[r], v_h[:n])
            delta = jnp.sum(prob * dp, axis=1, keepdims=True)
            ds = (prob * (dp - delta)).astype(BF16)
            dq_s[r, :] = dot_nn(ds, kq[:n])
            dk_part = dot_tn(kq[r], ds)
            if step == 0:
                dkt_s[...] = dk_part
            else:
                dkt_s[:, :n] += dk_part
            dvt_s[:, :n] += dot_tn(do_h[r], prob_low)

        dqk = jnp.where(low, dq_s[...], dkt_s[...].T)
        dqk = rope_mix(dqk, (c_ref[...], s1_ref[...], s2_ref[...]), -1)
        dqk_s[:, pl.ds(pl.multiple_of(t * PAIR, PAIR), PAIR)] = dqk.astype(BF16)

        @pl.when(odd == 1)
        def _():
            at = pl.ds(pl.multiple_of(p * PAIR, PAIR), PAIR)
            dv_s[:, at] = dvt_s[...].T.astype(BF16)
            o_s[:, at] = oacc_s[...].astype(BF16)

        return carry

    lax.fori_loop(0, heads, one_head, 0)

    @pl.when(pl.program_id(0) == 0)
    def _():
        y_ref[...] = jnp.zeros_like(y_ref)
        dx_ref[...] = jnp.zeros_like(dx_ref)

    dqk_all = dqk_s[...]
    dv_all = dv_s[...]
    o_all = o_s[...]
    y_ref[...] += dot_nt(o_all, wo)
    dx_ref[...] += dot_nt(dqk_all, wqk) + dot_nt(dv_all, wv)
    gw_ref[:, :nqk] = dot_nn(xt_ref[...], dqk_all).astype(BF16)
    gw_ref[:, nqk : nqk + nv] = dot_nn(xt_ref[...], dv_all).astype(BF16)
    gw_ref[:, nqk + nv :] = dot_nn(dyt_ref[...], o_all).astype(BF16)
    dbqk_ref[...] = jnp.sum(dqk_all.astype(F32), axis=0, keepdims=True)
    dbv_ref[...] = jnp.sum(dv_all.astype(F32), axis=0, keepdims=True)


def mlp_kernel(
    x_ref, xt_ref, dy_ref, dyt_ref, w_ref, b_ref, y_ref, dx_ref, gw_ref, db_ref, g_s, dh_s
):
    width = w_ref.shape[1] // 2
    wu = w_ref[:, :width]
    wd = w_ref[:, width:]

    @pl.when(pl.program_id(0) == 0)
    def _():
        y_ref[...] = jnp.zeros_like(y_ref)
        dx_ref[...] = jnp.zeros_like(dx_ref)

    total = jnp.zeros((1, width), F32)
    for i in range(SEQ_LEN // M_ROWS):
        r = slice(i * M_ROWS, (i + 1) * M_ROWS)
        h = dot_nn(x_ref[r, :], wu) + b_ref[...]
        dg = dot_nn(dy_ref[r, :], wd)
        phi = 0.5 + 0.5 * lax.erf(h * (0.5**0.5))
        g_s[r, :] = (h * phi).astype(BF16)
        slope = phi + h * (jnp.exp(h * h * -0.5) * 0.3989422804014327)
        dh = (dg * slope).astype(BF16)
        dh_s[r, :] = dh
        total += jnp.sum(dh.astype(F32), axis=0, keepdims=True)
        y_ref[r, :] += dot_nt(g_s[r, :], wd)
        dx_ref[r, :] += dot_nt(dh, wu)
    gw_ref[:, :width] = dot_nn(xt_ref[...], dh_s[...]).astype(BF16)
    gw_ref[:, width:] = dot_nn(dyt_ref[...], g_s[...]).astype(BF16)
    db_ref[...] = total


def last_kernel(
    x_ref, dy_ref, ya_ref, ym_ref, da_ref, dm_ref, gain_ref, bias_ref, out_ref, dx_ref, sums_ref
):
    x = x_ref[...].astype(F32)
    dy = dy_ref[...].astype(F32)
    normed, inverse = layer_stats(x)
    out_ref[...] = (x + (ya_ref[...] + ym_ref[...]) + bias_ref[0:1] + bias_ref[1:2]).astype(BF16)
    da = da_ref[...]
    dm = dm_ref[...]
    e = da * gain_ref[0:1] + dm * gain_ref[1:2]
    dx_ref[...] = dy + inverse * (
        e - jnp.mean(e, axis=1, keepdims=True) - normed * jnp.mean(e * normed, axis=1, keepdims=True)
    )

    @pl.when(pl.program_id(0) == 0)
    def _():
        sums_ref[...] = jnp.zeros_like(sums_ref)

    sums_ref[0:1] += jnp.sum(da * normed, axis=0, keepdims=True)
    sums_ref[1:2] += jnp.sum(dm * normed, axis=0, keepdims=True)
    sums_ref[2:3] += jnp.sum(da, axis=0, keepdims=True)
    sums_ref[3:4] += jnp.sum(dm, axis=0, keepdims=True)


def params():
    return pltpu.CompilerParams(
        dimension_semantics=("arbitrary",), vmem_limit_bytes=VMEM
    )


def whole(shape):
    return pl.BlockSpec(shape, lambda *_: (0,) * len(shape), pipeline_mode=pl.Buffered(1))


def whole_out(shape):
    return pl.BlockSpec(shape, lambda *_: (0,) * len(shape))


def run_norm(tokens, cotangent, gains, biases):
    rows, d = tokens.shape
    by_row = pl.BlockSpec((N_ROWS, d), lambda i: (i, 0))
    by_col = pl.BlockSpec((d, N_ROWS), lambda i: (0, i))
    flat = jax.ShapeDtypeStruct((rows, d), BF16)
    turned = jax.ShapeDtypeStruct((d, rows), BF16)
    return pl.pallas_call(
        norm_kernel,
        grid=(rows // N_ROWS,),
        in_specs=[by_row, by_row, whole((2, d)), whole((2, d))],
        out_specs=[by_row, by_row, by_col, by_col, by_col, whole_out((1, d))],
        out_shape=[flat, flat, turned, turned, turned, jax.ShapeDtypeStruct((1, d), F32)],
        compiler_params=params(),
        name="norm",
    )(tokens, cotangent, gains, biases)


def run_attn(x, xt, dy, dyt, w, bqk, bv, tables, heads):
    rows, d = x.shape
    nqk, nv = heads * PAIR, heads * HEAD_DIM
    width = nqk + 2 * nv
    chunks = w.shape[1] // width
    per = lambda n: pl.BlockSpec((1, n), lambda j: (0, j))
    half = (heads // 2, rows, PAIR)
    return pl.pallas_call(
        functools.partial(attn_kernel, heads),
        grid=(chunks,),
        in_specs=[
            whole((rows, d)),
            whole((d, rows)),
            whole((rows, d)),
            whole((d, rows)),
            pl.BlockSpec((d, width), lambda j: (0, j)),
            per(nqk),
            per(nv),
        ]
        + [whole((rows, PAIR))] * 3,
        out_specs=[
            whole_out((rows, d)),
            whole_out((rows, d)),
            pl.BlockSpec((d, width), lambda j: (0, j)),
            per(nqk),
            per(nv),
        ],
        out_shape=[
            jax.ShapeDtypeStruct((rows, d), F32),
            jax.ShapeDtypeStruct((rows, d), F32),
            jax.ShapeDtypeStruct((d, chunks * width), BF16),
            jax.ShapeDtypeStruct((1, chunks * nqk), F32),
            jax.ShapeDtypeStruct((1, chunks * nv), F32),
        ],
        scratch_shapes=[
            pltpu.VMEM((heads, rows, PAIR), BF16),
            pltpu.VMEM(half, BF16),
            pltpu.VMEM(half, BF16),
            pltpu.VMEM((rows, nqk), BF16),
            pltpu.VMEM((rows, nv), BF16),
            pltpu.VMEM((rows, nv), BF16),
            pltpu.VMEM((rows, PAIR), F32),
            pltpu.VMEM((PAIR, rows), F32),
            pltpu.VMEM((PAIR, rows), F32),
            pltpu.VMEM((rows, PAIR), F32),
        ],
        compiler_params=params(),
        name="attention",
    )(x, xt, dy, dyt, w, bqk, bv, *tables)


def run_mlp(x, xt, dy, dyt, w, b, width):
    rows, d = x.shape
    chunks = w.shape[1] // (2 * width)
    return pl.pallas_call(
        mlp_kernel,
        grid=(chunks,),
        in_specs=[
            whole((rows, d)),
            whole((d, rows)),
            whole((rows, d)),
            whole((d, rows)),
            pl.BlockSpec((d, 2 * width), lambda j: (0, j)),
            pl.BlockSpec((1, width), lambda j: (0, j)),
        ],
        out_specs=[
            whole_out((rows, d)),
            whole_out((rows, d)),
            pl.BlockSpec((d, 2 * width), lambda j: (0, j)),
            pl.BlockSpec((1, width), lambda j: (0, j)),
        ],
        out_shape=[
            jax.ShapeDtypeStruct((rows, d), F32),
            jax.ShapeDtypeStruct((rows, d), F32),
            jax.ShapeDtypeStruct((d, chunks * 2 * width), BF16),
            jax.ShapeDtypeStruct((1, chunks * width), F32),
        ],
        scratch_shapes=[pltpu.VMEM((rows, width), BF16), pltpu.VMEM((rows, width), BF16)],
        compiler_params=params(),
        name="mlp",
    )(x, xt, dy, dyt, w, b)


def run_last(tokens, dy, ya, ym, da, dm, gains, branch_bias):
    rows, d = tokens.shape
    by_row = pl.BlockSpec((N_ROWS, d), lambda i: (i, 0))
    return pl.pallas_call(
        last_kernel,
        grid=(rows // N_ROWS,),
        in_specs=[by_row] * 6 + [whole((2, d)), whole((2, d))],
        out_specs=[by_row, by_row, whole_out((8, d))],
        out_shape=[
            jax.ShapeDtypeStruct((rows, d), BF16),
            jax.ShapeDtypeStruct((rows, d), F32),
            jax.ShapeDtypeStruct((8, d), F32),
        ],
        compiler_params=params(),
        name="last",
    )(tokens, dy, ya, ym, da, dm, gains, branch_bias)


def ring(x, size, shift):
    return lax.ppermute(x, "tensor", [(i, (i - shift) % size) for i in range(size)])


def flip(x, size, bit):
    return lax.ppermute(x, "dp", [(i, i ^ bit) for i in range(size)])


def bits_of(size):
    return [1 << b for b in range(size.bit_length() - 1)]


def gather_tensor(x, size):
    me = lax.axis_index("tensor")
    parts = jnp.stack([x] + [ring(x, size, s) for s in range(1, size)])
    return lax.dynamic_slice_in_dim(
        jnp.concatenate([parts, parts]), lax.rem(size - me, size), size, 0
    )


def gather_dp(x, size):
    me = lax.axis_index("dp")
    x = x[None]
    for bit in bits_of(size):
        other = flip(x, size, bit)
        mine_high = (me & bit) != 0
        x = jnp.concatenate([jnp.where(mine_high, other, x), jnp.where(mine_high, x, other)])
    return x


def sum_all(x, dp, tp):
    for bit in bits_of(dp):
        x = x + flip(x, dp, bit)
    parts = [ring(x, tp, s) for s in range(1, tp)]
    for part in parts:
        x = x + part
    return x


def scatter_tensor(x, size):
    me = lax.axis_index("tensor")
    total = lax.dynamic_index_in_dim(x, me, 0, keepdims=False).astype(F32)
    for s in range(1, size):
        to = lax.rem(me + s, size)
        sent = ring(lax.dynamic_index_in_dim(x, to, 0, keepdims=False), size, size - s)
        total = total + sent.astype(F32)
    return total


def rope_tables():
    positions = jnp.arange(SEQ_LEN, dtype=F32)
    frequency = 10000.0 ** (-2.0 * jnp.arange(ROT // 2, dtype=F32) / ROT)
    angles = positions[:, None] * frequency[None, :]
    cosine, sine = jnp.cos(angles), jnp.sin(angles)
    none = jnp.zeros_like(sine)
    rest = jnp.zeros((SEQ_LEN, HEAD_DIM - ROT), F32)
    c = jnp.concatenate([cosine, cosine, rest + 1.0], axis=1)
    s1 = jnp.concatenate([-sine, none, rest], axis=1)
    s2 = jnp.concatenate([none, sine, rest], axis=1)
    scale = HEAD_DIM**-0.5
    return [jnp.concatenate([u * scale, u], axis=1) for u in (c, s1, s2)]


def on_device(
    dp,
    tp,
    tokens,
    ln_gains,
    ln_biases,
    w_query,
    w_key,
    w_value,
    query_bias,
    key_bias,
    value_bias,
    w_output,
    w_up,
    up_bias,
    w_down,
    out_biases,
    cotangent,
):
    rows, d = tokens.shape
    own = w_query.shape[0]
    groups = w_query.shape[1] // HEAD_DIM
    hidden = w_up.shape[1]
    parts = hidden // FF_CHUNK
    nqk, nv = tp * PAIR, tp * HEAD_DIM
    a_width = nqk + 2 * nv
    f_width = tp * FF_CHUNK

    small = jnp.concatenate(
        [u.reshape(-1) for u in (ln_gains, ln_biases, out_biases, query_bias, key_bias, value_bias, up_bias)]
    )
    small = gather_dp(gather_tensor(small, tp), dp).astype(F32)
    n = ln_gains.shape[1]
    pick = lambda k: small[:, :, 2 * n * k : 2 * n * (k + 1)].reshape(dp, tp, 2, n).transpose(2, 0, 1, 3).reshape(2, d)
    gains, biases, branch_bias = pick(0), pick(1), pick(2)
    at = 6 * n
    vec = small[0]
    hq = groups * HEAD_DIM
    by_head = lambda k: vec[:, at + hq * k : at + hq * (k + 1)].reshape(tp, groups, HEAD_DIM).transpose(1, 0, 2)
    bqk = jnp.stack([by_head(0), by_head(1)], axis=2).reshape(1, -1)
    bv = by_head(2).reshape(1, -1)
    bu = vec[:, at + 3 * hq :].reshape(tp, parts, FF_CHUNK).transpose(1, 0, 2).reshape(1, -1)

    wa = jnp.stack([w.reshape(own, groups, HEAD_DIM) for w in (w_query, w_key, w_value, w_output.T)], axis=2)
    wf = jnp.stack([w.reshape(own, parts, FF_CHUNK) for w in (w_up, w_down.T)], axis=2)
    shard = jnp.concatenate([wa.reshape(own, -1), wf.reshape(own, -1)], axis=1)
    full = gather_tensor(shard, tp)
    na = wa[0].size
    fa = full[:, :, :na].reshape(tp, own, groups, 4, HEAD_DIM).transpose(1, 2, 0, 3, 4)
    fqk = fa[:, :, :, :2].reshape(own, groups, nqk)
    fv = fa[:, :, :, 2].reshape(own, groups, nv)
    fo = fa[:, :, :, 3].reshape(own, groups, nv)
    fa = jnp.concatenate([fqk, fv, fo], axis=2).reshape(own, groups * a_width)
    ff = full[:, :, na:].reshape(tp, own, parts, 2, FF_CHUNK).transpose(1, 2, 3, 0, 4)
    ff = ff.reshape(own, parts * 2 * f_width)
    fa = lax.all_gather(fa, "dp", axis=0, tiled=True)
    ff = lax.all_gather(ff, "dp", axis=0, tiled=True)

    attn_in, mlp_in, attn_t, mlp_t, dy_t, dy_sum = run_norm(tokens, cotangent, gains, biases)
    tables = rope_tables()
    ya, da, ga, dbqk, dbv = run_attn(attn_in, attn_t, cotangent, dy_t, fa, bqk, bv, tables, tp)
    ym, dm, gf, dbu = run_mlp(mlp_in, mlp_t, cotangent, dy_t, ff, bu, f_width)
    block_out, grad_tokens, sums = run_last(tokens, cotangent, ya, ym, da, dm, gains, branch_bias)

    ga = lax.psum_scatter(ga, "dp", scatter_dimension=0, tiled=True)
    gf = lax.psum_scatter(gf, "dp", scatter_dimension=0, tiled=True)
    ga = ga.reshape(own, groups, a_width)
    gqk = ga[:, :, :nqk].reshape(own, groups, tp, 2, HEAD_DIM)
    gv = ga[:, :, nqk : nqk + nv].reshape(own, groups, tp, 1, HEAD_DIM)
    go = ga[:, :, nqk + nv :].reshape(own, groups, tp, 1, HEAD_DIM)
    ga = jnp.concatenate([gqk, gv, go], axis=3).transpose(2, 0, 1, 3, 4).reshape(tp, own, -1)
    gf = gf.reshape(own, parts, 2, tp, FF_CHUNK).transpose(3, 0, 1, 2, 4).reshape(tp, own, -1)
    grads = scatter_tensor(jnp.concatenate([ga, gf], axis=2), tp)
    ga = grads[:, :na].reshape(own, groups, 4, HEAD_DIM)
    gf = grads[:, na:].reshape(own, parts, 2, FF_CHUNK)
    grad_w_query, grad_w_key, grad_w_value, grad_w_output = [
        ga[:, :, k].reshape(own, -1) for k in range(4)
    ]
    grad_w_up, grad_w_down = [gf[:, :, k].reshape(own, -1) for k in range(2)]

    vectors = jnp.concatenate(
        [sums[:4].reshape(-1), dy_sum.reshape(-1), dbqk.reshape(-1), dbv.reshape(-1), dbu.reshape(-1)]
    )
    vectors = sum_all(vectors.reshape(-1, 128), dp, tp).reshape(-1)
    me = lax.axis_index("dp") * tp + lax.axis_index("tensor")
    rows5 = lax.dynamic_slice_in_dim(vectors[: 5 * d].reshape(5, d), me * n, n, 1)
    t = lax.axis_index("tensor")
    at = 5 * d
    vqk = vectors[at : at + groups * nqk].reshape(groups, tp, 2, HEAD_DIM)
    vv = vectors[at + groups * nqk : at + groups * (nqk + nv)].reshape(groups, tp, HEAD_DIM)
    vu = vectors[at + groups * (nqk + nv) :].reshape(parts, tp, FF_CHUNK)
    vqk = lax.dynamic_index_in_dim(vqk, t, 1, keepdims=False)
    grad_query_bias, grad_key_bias = vqk[:, 0].reshape(-1), vqk[:, 1].reshape(-1)
    grad_value_bias = lax.dynamic_index_in_dim(vv, t, 1, keepdims=False).reshape(-1)
    grad_up_bias = lax.dynamic_index_in_dim(vu, t, 1, keepdims=False).reshape(-1)
    return (
        block_out,
        grad_tokens,
        rows5[0:2],
        rows5[2:4],
        grad_w_query,
        grad_w_key,
        grad_w_value,
        grad_query_bias,
        grad_key_bias,
        grad_value_bias,
        grad_w_output.T,
        grad_w_up,
        grad_up_bias,
        grad_w_down.T,
        jnp.concatenate([rows5[4:5], rows5[4:5]]),
    )


def solution(mesh):
    rows = P(("dp", "tensor"), None)
    cols = P(None, ("dp", "tensor"))
    wide, tall, vec = P("dp", "tensor"), P("tensor", "dp"), P("tensor")
    return jax.shard_map(
        functools.partial(on_device, mesh.shape["dp"], mesh.shape["tensor"]),
        mesh=mesh,
        in_specs=(rows, cols, cols, wide, wide, wide, vec, vec, vec, tall, wide, vec, tall, cols, rows),
        out_specs=(
            rows, rows, cols, cols, wide, wide, wide, vec, vec, vec, tall, wide, vec, tall, cols,
        ),
        check_vma=False,
    )
```

```python
import functools

import jax
import jax.numpy as jnp
from jax import lax
from jax.experimental import pallas as pl
from jax.experimental.pallas import tpu as pltpu
from jax.sharding import PartitionSpec as P

HEAD_DIM = 64
ROT = 16
SEQ_LEN = 1024
EPSILON = 1e-05
PAIR = 2 * HEAD_DIM
Q_ROWS = 256
M_ROWS = 512
N_ROWS = 256
FF_CHUNK = 256
VMEM = 60 * 1024 * 1024
F32 = jnp.float32
BF16 = jnp.bfloat16


def dot_nn(a, b):
    return jnp.dot(a, b, preferred_element_type=F32)


def dot_nt(a, b):
    return lax.dot_general(a, b, (((1,), (1,)), ((), ())), preferred_element_type=F32)


def dot_tn(a, b):
    return lax.dot_general(a, b, (((0,), (0,)), ((), ())), preferred_element_type=F32)


def layer_stats(rows):
    center = rows - jnp.mean(rows, axis=1, keepdims=True)
    inverse = lax.rsqrt(jnp.mean(center * center, axis=1, keepdims=True) + EPSILON)
    return center * inverse, inverse


def norm_kernel(
    steps,
    me_ref,
    x_ref,
    dy_ref,
    gain_ref,
    bias_ref,
    a_ref,
    m_ref,
    at_ref,
    dyt_ref,
    mt_ref,
    dyp_ref,
    sum_ref,
):
    normed, _ = layer_stats(x_ref[...].astype(F32))
    a = normed * gain_ref[0:1] + bias_ref[0:1]
    m = normed * gain_ref[1:2] + bias_ref[1:2]
    dy = dy_ref[...].astype(F32)
    a_ref[...] = a.astype(BF16)
    m_ref[...] = m.astype(BF16)
    at_ref[...] = a.T.astype(BF16)
    mt = m.T.astype(BF16)
    dyt = dy.T.astype(BF16)
    dyt_ref[...] = dyt
    if steps is None:
        mt_ref[...] = mt
        dyp_ref[...] = dyt
    else:
        count = 1 << len(steps[0])
        own = mt.shape[0] // count
        for ref, value, order in ((mt_ref, mt, steps[0]), (dyp_ref, dyt, steps[1])):
            for owner in range(count):
                place = place_of(owner ^ me_ref[0], order)
                ref[pl.ds(pl.multiple_of(place * own, own), own), :] = value[
                    owner * own : (owner + 1) * own
                ]

    @pl.when(pl.program_id(0) == 0)
    def _():
        sum_ref[...] = jnp.zeros_like(sum_ref)

    sum_ref[...] += jnp.sum(dy, axis=0, keepdims=True)


def place_of(relative, order):
    place = 0
    for bit in order:
        place = place * 2 + ((relative // bit) % 2)
    return place


def rope_mix(u, tables, sign):
    c, s1, s2 = tables
    turned = pltpu.roll(u, PAIR - ROT // 2, 1) * s1 + pltpu.roll(u, ROT // 2, 1) * s2
    return u * c + turned if sign > 0 else u * c - turned


def attn_kernel(
    heads,
    x_ref,
    xt_ref,
    dy_ref,
    dyt_ref,
    w_ref,
    bqk_ref,
    bv_ref,
    c_ref,
    s1_ref,
    s2_ref,
    o_s,
    dqk_s,
    dv_s,
    gw_ref,
    dbqk_ref,
    dbv_ref,
    qk_s,
    v_s,
    do_s,
    dq_s,
    dkt_s,
    dvt_s,
    oacc_s,
    s_s,
    dp_s,
    p_s,
    ds_s,
):
    nqk = heads * PAIR
    nv = heads * HEAD_DIM
    wqk = w_ref[:, :nqk]
    wv = w_ref[:, nqk : nqk + nv]
    wo = w_ref[:, nqk + nv :]
    qk = dot_nn(x_ref[...], wqk) + bqk_ref[...]
    for t in range(heads):
        u = qk[:, t * PAIR : (t + 1) * PAIR]
        qk_s[t] = rope_mix(u, (c_ref[...], s1_ref[...], s2_ref[...]), 1).astype(BF16)
    v = (dot_nn(x_ref[...], wv) + bv_ref[...]).astype(BF16)
    do = dot_nn(dy_ref[...], wo).astype(BF16)
    for p in range(heads // 2):
        v_s[p] = v[:, p * PAIR : (p + 1) * PAIR]
        do_s[p] = do[:, p * PAIR : (p + 1) * PAIR]

    lane = lax.broadcasted_iota(jnp.int32, (1, PAIR), 1)
    low = lane < HEAD_DIM
    below = lax.broadcasted_iota(jnp.int32, (Q_ROWS, Q_ROWS), 0) >= lax.broadcasted_iota(
        jnp.int32, (Q_ROWS, Q_ROWS), 1
    )

    blocks = SEQ_LEN // Q_ROWS

    def one_pair(p, carry):
        v_p = v_s[p]
        do_p = do_s[p]
        for odd in range(2):
            t = p * 2 + odd
            mine = low if odd == 0 else lane >= HEAD_DIM
            qk_h = qk_s[t]
            kq = pltpu.roll(qk_h.astype(F32), HEAD_DIM, 1)
            kqt = kq.T.astype(BF16)
            kq = kq.astype(BF16)
            q_only = jnp.where(low, qk_h, jnp.zeros_like(qk_h))
            v_h = jnp.where(mine, v_p, jnp.zeros_like(v_p))
            do_h = jnp.where(mine, do_p, jnp.zeros_like(do_p))
            vt = v_h.T
            dot = do_h.T
            for j in range(blocks):
                c = slice(j * Q_ROWS, (j + 1) * Q_ROWS)
                s_s[odd, j * Q_ROWS :, c] = dot_nn(q_only[j * Q_ROWS :], kqt[:, c])
                dp_s[odd, j * Q_ROWS :, c] = dot_nn(do_h[j * Q_ROWS :], vt[:, c])
            for i in range(blocks):
                r = slice(i * Q_ROWS, (i + 1) * Q_ROWS)
                n = (i + 1) * Q_ROWS
                s = s_s[odd, r, :n]
                tail = jnp.where(below, s[:, n - Q_ROWS :], -1e30)
                s = tail if i == 0 else jnp.concatenate([s[:, : n - Q_ROWS], tail], axis=1)
                top = jnp.max(s, axis=1, keepdims=True)
                e = jnp.exp(s - top)
                total = jnp.sum(e, axis=1, keepdims=True)
                prob = e * (1.0 / total)
                p_s[odd, r, :n] = prob.astype(BF16)
                dp = dp_s[odd, r, :n]
                delta = jnp.sum(prob * dp, axis=1, keepdims=True)
                ds_s[odd, r, :n] = (prob * (dp - delta)).astype(BF16)
            for j in range(blocks):
                c = slice(j * Q_ROWS, (j + 1) * Q_ROWS)
                prob_low = p_s[odd, j * Q_ROWS :, c]
                ds = ds_s[odd, j * Q_ROWS :, c]
                o_part = dot_nn(prob_low, v_h[c])
                dq_part = dot_nn(ds, kq[c])
                if odd == 0 and j == 0:
                    oacc_s[...] = o_part
                else:
                    oacc_s[j * Q_ROWS :, :] += o_part
                if j == 0:
                    dq_s[odd] = dq_part
                else:
                    dq_s[odd, j * Q_ROWS :, :] += dq_part
                dkt_s[odd, :, c] = dot_nn(kqt[:, j * Q_ROWS :], ds)
                dv_part = dot_nn(dot[:, j * Q_ROWS :], prob_low)
                if odd == 0:
                    dvt_s[:, c] = dv_part
                else:
                    dvt_s[:, c] += dv_part
            dqk = jnp.where(low, dq_s[odd], dkt_s[odd].T)
            dqk = rope_mix(dqk, (c_ref[...], s1_ref[...], s2_ref[...]), -1)
            dqk_s[:, pl.ds(pl.multiple_of(t * PAIR, PAIR), PAIR)] = dqk.astype(BF16)
        at = pl.ds(pl.multiple_of(p * PAIR, PAIR), PAIR)
        dv_s[:, at] = dvt_s[...].T.astype(BF16)
        o_s[:, at] = oacc_s[...].astype(BF16)
        return carry

    lax.fori_loop(0, heads // 2, one_pair, 0)

    dqk_all = dqk_s[...]
    dv_all = dv_s[...]
    o_all = o_s[...]
    gw_ref[:, :nqk] = dot_nn(xt_ref[...], dqk_all).astype(BF16)
    gw_ref[:, nqk : nqk + nv] = dot_nn(xt_ref[...], dv_all).astype(BF16)
    gw_ref[:, nqk + nv :] = dot_nn(dyt_ref[...], o_all).astype(BF16)
    dbqk_ref[...] = jnp.sum(dqk_all.astype(F32), axis=0, keepdims=True)
    dbv_ref[...] = jnp.sum(dv_all.astype(F32), axis=0, keepdims=True)


def mlp_kernel(
    x_ref, xt_ref, dy_ref, dyt_ref, wu_ref, wd_ref, b_ref, g_ref, dh_ref, uk_ref, us_ref, dk_ref, ds_ref, db_ref
):
    half = xt_ref.shape[0] // 2
    h = dot_nn(x_ref[...], wu_ref[...]) + b_ref[...]
    dg = dot_nn(dy_ref[...], wd_ref[...])
    phi = 0.5 + 0.5 * lax.erf(h * (0.5**0.5))
    g_ref[...] = (h * phi).astype(BF16)
    slope = phi + h * (jnp.exp(h * h * -0.5) * 0.3989422804014327)
    dh = (dg * slope).astype(BF16)
    dh_ref[...] = dh
    db_ref[...] = jnp.sum(dh.astype(F32), axis=0, keepdims=True)
    us_ref[...] = dot_nn(xt_ref[half:, :], dh).astype(BF16)
    uk_ref[...] = dot_nn(xt_ref[:half, :], dh).astype(BF16)
    g = g_ref[...]
    ds_ref[...] = dot_nn(dyt_ref[half:, :], g).astype(BF16)
    dk_ref[...] = dot_nn(dyt_ref[:half, :], g).astype(BF16)


def fold_kernel(uk_ref, ur_ref, dk_ref, dr_ref, *out_refs):
    half = uk_ref.shape[0] // 2
    for keep, got, outs in ((uk_ref, ur_ref, out_refs[:2]), (dk_ref, dr_ref, out_refs[2:])):
        outs[1][...] = (keep[half:, :].astype(F32) + got[half:, :].astype(F32)).astype(BF16)
        outs[0][...] = (keep[:half, :].astype(F32) + got[:half, :].astype(F32)).astype(BF16)


def split_kernel(me_ref, uk_ref, ur_ref, dk_ref, dr_ref, *out_refs):
    size = len(out_refs)
    width = uk_ref.shape[1] // size
    for shift, out in enumerate(out_refs):
        at = pl.ds(pl.multiple_of(lax.rem(me_ref[0] + shift, size) * width, width), width)
        out[:, :width] = (uk_ref[:, at].astype(F32) + ur_ref[:, at].astype(F32)).astype(BF16)
        out[:, width:] = (dk_ref[:, at].astype(F32) + dr_ref[:, at].astype(F32)).astype(BF16)


def out_kernel(parts_a, parts_f, x_ref, bias_ref, o_ref, *refs):
    wo = refs[:parts_a]
    g = refs[parts_a : parts_a + parts_f]
    wd = refs[parts_a + parts_f : -1]
    width = wo[0].shape[1]
    total = x_ref[...].astype(F32) + bias_ref[0:1] + bias_ref[1:2]
    for j in range(parts_a):
        total += dot_nt(o_ref[:, j * width : (j + 1) * width], wo[j][...])
    for c in range(parts_f):
        total += dot_nt(g[c][...], wd[c][...])
    refs[-1][...] = total.astype(BF16)


def back_mlp_kernel(parts, *refs):
    total = dot_nt(refs[0][...], refs[parts][...])
    for c in range(1, parts):
        total += dot_nt(refs[c][...], refs[parts + c][...])
    refs[-1][...] = total


def last_kernel(parts, x_ref, dy_ref, dm_ref, gain_ref, dqk_ref, dv_ref, *refs):
    wqk, wv = refs[:parts], refs[parts : 2 * parts]
    dx_ref, sums_ref = refs[2 * parts :]
    nqk, nv = wqk[0].shape[1], wv[0].shape[1]
    da = dot_nt(dqk_ref[:, :nqk], wqk[0][...])
    for j in range(1, parts):
        da += dot_nt(dqk_ref[:, j * nqk : (j + 1) * nqk], wqk[j][...])
    for j in range(parts):
        da += dot_nt(dv_ref[:, j * nv : (j + 1) * nv], wv[j][...])
    dm = dm_ref[...]
    normed, inverse = layer_stats(x_ref[...].astype(F32))
    e = da * gain_ref[0:1] + dm * gain_ref[1:2]
    dx_ref[...] = dy_ref[...].astype(F32) + inverse * (
        e - jnp.mean(e, axis=1, keepdims=True) - normed * jnp.mean(e * normed, axis=1, keepdims=True)
    )

    @pl.when(pl.program_id(0) == 0)
    def _():
        sums_ref[...] = jnp.zeros_like(sums_ref)

    sums_ref[0:1] += jnp.sum(da * normed, axis=0, keepdims=True)
    sums_ref[1:2] += jnp.sum(dm * normed, axis=0, keepdims=True)
    sums_ref[2:3] += jnp.sum(da, axis=0, keepdims=True)
    sums_ref[3:4] += jnp.sum(dm, axis=0, keepdims=True)


def params():
    return pltpu.CompilerParams(
        dimension_semantics=("arbitrary",), vmem_limit_bytes=VMEM
    )


def whole(shape):
    return pl.BlockSpec(shape, lambda *_: (0,) * len(shape), pipeline_mode=pl.Buffered(1))


def whole_out(shape):
    return pl.BlockSpec(shape, lambda *_: (0,) * len(shape))


def cost(flops, moved, special=0):
    return pl.CostEstimate(flops=flops, bytes_accessed=moved, transcendentals=special)


def scalar_in():
    return pl.BlockSpec(memory_space=pltpu.SMEM)


def run_norm(me, tokens, cotangent, gains, biases, steps):
    rows, d = tokens.shape
    by_row = pl.BlockSpec((N_ROWS, d), lambda i: (i, 0))
    by_col = pl.BlockSpec((d, N_ROWS), lambda i: (0, i))
    flat = jax.ShapeDtypeStruct((rows, d), BF16)
    turned = jax.ShapeDtypeStruct((d, rows), BF16)
    return pl.pallas_call(
        functools.partial(norm_kernel, steps),
        grid=(rows // N_ROWS,),
        in_specs=[scalar_in(), by_row, by_row, whole((2, d)), whole((2, d))],
        out_specs=[by_row, by_row, by_col, by_col, by_col, by_col, whole_out((1, d))],
        out_shape=[flat, flat, turned, turned, turned, turned, jax.ShapeDtypeStruct((1, d), F32)],
        compiler_params=params(),
        cost_estimate=cost(40 * rows * d, 16 * rows * d),
        name="norm",
    )(me, tokens, cotangent, gains, biases)


def run_attn(x, xt, dy, dyt, w, bqk, bv, tables, heads):
    rows, d = x.shape
    nqk, nv = heads * PAIR, heads * HEAD_DIM
    width = nqk + 2 * nv
    chunks = w.shape[1] // width
    per = lambda n: pl.BlockSpec((1, n), lambda j: (0, j))
    tall = lambda n: pl.BlockSpec((rows, n), lambda j: (0, j))
    half = (heads // 2, rows, PAIR)
    return pl.pallas_call(
        functools.partial(attn_kernel, heads),
        grid=(chunks,),
        in_specs=[
            whole((rows, d)),
            whole((d, rows)),
            whole((rows, d)),
            whole((d, rows)),
            pl.BlockSpec((d, width), lambda j: (0, j)),
            per(nqk),
            per(nv),
        ]
        + [whole((rows, PAIR))] * 3,
        out_specs=[
            tall(nv),
            tall(nqk),
            tall(nv),
            pl.BlockSpec((d, width), lambda j: (0, j)),
            per(nqk),
            per(nv),
        ],
        out_shape=[
            jax.ShapeDtypeStruct((rows, chunks * nv), BF16),
            jax.ShapeDtypeStruct((rows, chunks * nqk), BF16),
            jax.ShapeDtypeStruct((rows, chunks * nv), BF16),
            jax.ShapeDtypeStruct((d, chunks * width), BF16),
            jax.ShapeDtypeStruct((1, chunks * nqk), F32),
            jax.ShapeDtypeStruct((1, chunks * nv), F32),
        ],
        scratch_shapes=[
            pltpu.VMEM((heads, rows, PAIR), BF16),
            pltpu.VMEM(half, BF16),
            pltpu.VMEM(half, BF16),
            pltpu.VMEM((2, rows, PAIR), F32),
            pltpu.VMEM((2, PAIR, rows), F32),
            pltpu.VMEM((PAIR, rows), F32),
            pltpu.VMEM((rows, PAIR), F32),
            pltpu.VMEM((2, rows, rows), F32),
            pltpu.VMEM((2, rows, rows), F32),
            pltpu.VMEM((2, rows, rows), BF16),
            pltpu.VMEM((2, rows, rows), BF16),
        ],
        compiler_params=params(),
        cost_estimate=cost(
            4 * rows * d * chunks * width + 24 * chunks * heads * rows * rows * PAIR,
            20 * rows * d,
            chunks * heads * rows * rows,
        ),
        name="attention",
    )(x, xt, dy, dyt, w, bqk, bv, *tables)


def run_mlp(x, xt, dy, dyt, w, b, heads, c):
    rows, d = x.shape
    n = FF_CHUNK
    width = heads * n
    half = d // 2
    by = lambda r, dt: jax.ShapeDtypeStruct((r, width), dt)
    tall = lambda r: pl.BlockSpec((r, n), lambda t: (0, t))
    return pl.pallas_call(
        mlp_kernel,
        grid=(heads,),
        in_specs=[
            whole((rows, d)),
            whole((d, rows)),
            whole((rows, d)),
            whole((d, rows)),
            pl.BlockSpec((d, n), lambda t: (0, 2 * c * heads + t)),
            pl.BlockSpec((d, n), lambda t: (0, (2 * c + 1) * heads + t)),
            pl.BlockSpec((1, n), lambda t: (0, c * heads + t)),
        ],
        out_specs=[tall(rows), tall(rows)] + [tall(half)] * 4 + [tall(1)],
        out_shape=[by(rows, BF16), by(rows, BF16)] + [by(half, BF16)] * 4 + [by(1, F32)],
        compiler_params=params(),
        cost_estimate=cost(8 * rows * d * width, 4 * rows * d * 5, rows * width),
        name="mlp",
    )(x, xt, dy, dyt, w, w, b)


def full_spec(x):
    return pl.BlockSpec(x.shape, lambda *_: (0,) * x.ndim)


def run_fold(uk, ur, dk, dr):
    rows, n = uk.shape
    out = jax.ShapeDtypeStruct((rows // 2, n), BF16)
    return pl.pallas_call(
        fold_kernel,
        out_shape=[out] * 4,
        compiler_params=pltpu.CompilerParams(vmem_limit_bytes=VMEM // 2),
        cost_estimate=cost(2 * rows * n, 12 * rows * n),
        name="fold",
    )(uk, ur, dk, dr)


def run_split(me, uk, ur, dk, dr, size):
    rows, n = uk.shape
    out = jax.ShapeDtypeStruct((rows, 2 * n // size), BF16)
    return pl.pallas_call(
        split_kernel,
        in_specs=[scalar_in()] + [full_spec(uk)] * 4,
        out_shape=[out] * size,
        compiler_params=pltpu.CompilerParams(vmem_limit_bytes=VMEM // 2),
        cost_estimate=cost(2 * rows * n, 12 * rows * n),
        name="split",
    )(me, uk, ur, dk, dr)


def row_call(kernel, name, rows, d, row_ins, fixed_ins, weights, outs, sums, flops):
    in_specs = [pl.BlockSpec((M_ROWS, u.shape[1]), lambda i: (i, 0)) for u in row_ins[0]]
    in_specs += [whole(u.shape) for u in fixed_ins]
    in_specs += [pl.BlockSpec((M_ROWS, u.shape[1]), lambda i: (i, 0)) for u in row_ins[1]]
    args = list(row_ins[0]) + list(fixed_ins) + list(row_ins[1])
    for kind in weights:
        if isinstance(kind, tuple):
            u, n, at = kind
            in_specs.append(
                pl.BlockSpec((d, n), lambda i, at=at: (0, at), pipeline_mode=pl.Buffered(1))
            )
            args.append(u)
        else:
            in_specs.append(pl.BlockSpec((M_ROWS, kind.shape[1]), lambda i: (i, 0)))
            args.append(kind)
    out_specs = [pl.BlockSpec((M_ROWS, d), lambda i: (i, 0)) for _ in outs]
    out_shape = [jax.ShapeDtypeStruct((rows, d), dt) for dt in outs]
    if sums:
        out_specs.append(whole_out((8, d)))
        out_shape.append(jax.ShapeDtypeStruct((8, d), F32))
    return pl.pallas_call(
        kernel,
        grid=(rows // M_ROWS,),
        in_specs=in_specs,
        out_specs=out_specs,
        out_shape=out_shape,
        compiler_params=params(),
        cost_estimate=cost(flops, 12 * rows * d),
        name=name,
    )(*args)


def ring(x, size, shift):
    return lax.ppermute(x, "tensor", [(i, (i - shift) % size) for i in range(size)])


def flip(x, size, bit):
    return lax.ppermute(x, "dp", [(i, i ^ bit) for i in range(size)])


def bits_of(size):
    return [1 << b for b in range(size.bit_length() - 1)]


def gather_tensor(x, size):
    me = lax.axis_index("tensor")
    parts = jnp.stack([x] + [ring(x, size, s) for s in range(1, size)])
    return lax.dynamic_slice_in_dim(
        jnp.concatenate([parts, parts]), lax.rem(size - me, size), size, 0
    )


def gather_dp(x, size):
    me = lax.axis_index("dp")
    x = x[None]
    for bit in bits_of(size):
        other = flip(x, size, bit)
        mine_high = (me & bit) != 0
        x = jnp.concatenate([jnp.where(mine_high, other, x), jnp.where(mine_high, x, other)])
    return x


def sum_all(x, dp, tp):
    for bit in bits_of(dp):
        x = x + flip(x, dp, bit)
    parts = [ring(x, tp, s) for s in range(1, tp)]
    for part in parts:
        x = x + part
    return x


def scatter_tensor(x, size):
    me = lax.axis_index("tensor")
    total = lax.dynamic_index_in_dim(x, me, 0, keepdims=False).astype(F32)
    for s in range(1, size):
        to = lax.rem(me + s, size)
        sent = ring(lax.dynamic_index_in_dim(x, to, 0, keepdims=False), size, size - s)
        total = total + sent.astype(F32)
    return total


def rope_tables():
    positions = jnp.arange(SEQ_LEN, dtype=F32)
    frequency = 10000.0 ** (-2.0 * jnp.arange(ROT // 2, dtype=F32) / ROT)
    angles = positions[:, None] * frequency[None, :]
    cosine, sine = jnp.cos(angles), jnp.sin(angles)
    none = jnp.zeros_like(sine)
    rest = jnp.zeros((SEQ_LEN, HEAD_DIM - ROT), F32)
    c = jnp.concatenate([cosine, cosine, rest + 1.0], axis=1)
    s1 = jnp.concatenate([-sine, none, rest], axis=1)
    s2 = jnp.concatenate([none, sine, rest], axis=1)
    scale = HEAD_DIM**-0.5
    return [jnp.concatenate([u * scale, u], axis=1) for u in (c, s1, s2)]


def on_device(
    dp,
    tp,
    tokens,
    ln_gains,
    ln_biases,
    w_query,
    w_key,
    w_value,
    query_bias,
    key_bias,
    value_bias,
    w_output,
    w_up,
    up_bias,
    w_down,
    out_biases,
    cotangent,
):
    rows, d = tokens.shape
    own = w_query.shape[0]
    groups = w_query.shape[1] // HEAD_DIM
    hidden = w_up.shape[1]
    parts = hidden // FF_CHUNK
    nqk, nv = tp * PAIR, tp * HEAD_DIM
    a_width = nqk + 2 * nv
    f_width = tp * FF_CHUNK

    small = jnp.concatenate(
        [u.reshape(-1) for u in (ln_gains, ln_biases, out_biases, query_bias, key_bias, value_bias, up_bias)]
    )
    small = gather_dp(gather_tensor(small, tp), dp).astype(F32)
    n = ln_gains.shape[1]
    pick = lambda k: small[:, :, 2 * n * k : 2 * n * (k + 1)].reshape(dp, tp, 2, n).transpose(2, 0, 1, 3).reshape(2, d)
    gains, biases, branch_bias = pick(0), pick(1), pick(2)
    at = 6 * n
    vec = small[0]
    hq = groups * HEAD_DIM
    by_head = lambda k: vec[:, at + hq * k : at + hq * (k + 1)].reshape(tp, groups, HEAD_DIM).transpose(1, 0, 2)
    bqk = jnp.stack([by_head(0), by_head(1)], axis=2).reshape(1, -1)
    bv = by_head(2).reshape(1, -1)
    bu = vec[:, at + 3 * hq :].reshape(tp, parts, FF_CHUNK).transpose(1, 0, 2).reshape(1, -1)

    wa = jnp.stack([w.reshape(own, groups, HEAD_DIM) for w in (w_query, w_key, w_value, w_output.T)], axis=2)
    na = wa[0].size
    fa = gather_tensor(wa.reshape(own, na), tp)
    wf = jnp.stack([w.reshape(own, parts, FF_CHUNK) for w in (w_up, w_down.T)], axis=2)
    wf, fa = lax.optimization_barrier((wf, fa))
    fa = fa.reshape(tp, own, groups, 4, HEAD_DIM).transpose(1, 2, 0, 3, 4)
    fqk = fa[:, :, :, :2].reshape(own, groups, nqk)
    fv = fa[:, :, :, 2].reshape(own, groups, nv)
    fo = fa[:, :, :, 3].reshape(own, groups, nv)
    fa = jnp.concatenate([fqk, fv, fo], axis=2).reshape(own, groups * a_width)
    fa = lax.all_gather(fa, "dp", axis=0, tiled=True)
    ff = gather_tensor(wf.reshape(own, -1), tp)
    ff = ff.reshape(tp, own, parts, 2, FF_CHUNK).transpose(1, 2, 3, 0, 4)
    ff = ff.reshape(own, parts * 2 * f_width)
    ff = lax.all_gather(ff, "dp", axis=0, tiled=True)

    me_dp = lax.axis_index("dp").astype(jnp.int32).reshape(1)
    me_tp = lax.axis_index("tensor").astype(jnp.int32).reshape(1)
    bits = bits_of(dp)
    steps = (bits, bits[:1] + bits[:0:-1]) if own % 16 == 0 and len(bits) == 3 else None
    attn_in, mlp_in, attn_t, dy_t, mlp_tp, dy_tp, dy_sum = run_norm(
        me_dp, tokens, cotangent, gains, biases, steps
    )
    tables = rope_tables()
    o, dqk, dv, ga, dbqk, dbv = run_attn(
        attn_in, attn_t, cotangent, dy_t, fa, bqk, bv, tables, tp
    )
    ga = lax.psum_scatter(ga, "dp", scatter_dimension=0, tiled=True)
    g, dh, dbu, pieces = [], [], [], []
    for c in range(parts):
        g_c, dh_c, uk, us, dk, ds, db = run_mlp(mlp_in, mlp_tp, cotangent, dy_tp, ff, bu, tp, c)
        g.append(g_c)
        dh.append(dh_c)
        dbu.append(db)
        if steps is None:
            join = lambda a, b: jnp.concatenate([a, b], axis=0)
            u = lax.psum_scatter(join(uk, us), "dp", scatter_dimension=0, tiled=True)
            w = lax.psum_scatter(join(dk, ds), "dp", scatter_dimension=0, tiled=True)
            both = jnp.stack([u.reshape(own, tp, FF_CHUNK), w.reshape(own, tp, FF_CHUNK)], axis=2)
            pieces.append(scatter_tensor(both.transpose(1, 0, 2, 3).reshape(tp, own, -1), tp))
            continue
        for at in range(2):
            ur, dr = flip(us, dp, steps[0][at]), flip(ds, dp, steps[1][at])
            uk, us, dk, ds = run_fold(uk, ur, dk, dr)
        ur, dr = flip(us, dp, steps[0][2]), flip(ds, dp, steps[1][2])
        split = run_split(me_tp, uk, ur, dk, dr, tp)
        total = split[0].astype(F32)
        for s in range(1, tp):
            total = total + ring(split[s], tp, tp - s).astype(F32)
        pieces.append(total)

    rows_d = 2 * rows * d
    (block_out,) = row_call(
        functools.partial(out_kernel, groups, parts),
        "forward_out",
        rows,
        d,
        ([tokens], [o]),
        [branch_bias],
        [(fa, nv, 4 * j + 3) for j in range(groups)] + g + [(ff, f_width, 2 * c + 1) for c in range(parts)],
        [BF16],
        False,
        rows_d * (groups * nv + parts * f_width),
    )
    (dm,) = row_call(
        functools.partial(back_mlp_kernel, parts),
        "back_mlp",
        rows,
        d,
        (dh, []),
        [],
        [(ff, f_width, 2 * c) for c in range(parts)],
        [F32],
        False,
        rows_d * parts * f_width,
    )
    grad_tokens, sums = row_call(
        functools.partial(last_kernel, groups),
        "last",
        rows,
        d,
        ([tokens, cotangent, dm], [dqk, dv]),
        [gains],
        [(fa, nqk, 2 * j) for j in range(groups)] + [(fa, nv, 4 * j + 2) for j in range(groups)],
        [F32],
        True,
        rows_d * groups * (nqk + nv),
    )

    ga = ga.reshape(own, groups, a_width)
    gqk = ga[:, :, :nqk].reshape(own, groups, tp, 2, HEAD_DIM)
    gv = ga[:, :, nqk : nqk + nv].reshape(own, groups, tp, 1, HEAD_DIM)
    go = ga[:, :, nqk + nv :].reshape(own, groups, tp, 1, HEAD_DIM)
    ga = jnp.concatenate([gqk, gv, go], axis=3).transpose(2, 0, 1, 3, 4).reshape(tp, own, -1)
    ga = scatter_tensor(ga, tp).reshape(own, groups, 4, HEAD_DIM)
    grad_w_query, grad_w_key, grad_w_value, grad_w_output = [
        ga[:, :, k].reshape(own, -1) for k in range(4)
    ]
    grad_w_up = jnp.concatenate([u[:, :FF_CHUNK] for u in pieces], axis=1)
    grad_w_down = jnp.concatenate([u[:, FF_CHUNK:] for u in pieces], axis=1)
    dbu = jnp.concatenate(dbu, axis=1)

    vectors = jnp.concatenate(
        [sums[:4].reshape(-1), dy_sum.reshape(-1), dbqk.reshape(-1), dbv.reshape(-1), dbu.reshape(-1)]
    )
    vectors = sum_all(vectors.reshape(-1, 128), dp, tp).reshape(-1)
    me = lax.axis_index("dp") * tp + lax.axis_index("tensor")
    rows5 = lax.dynamic_slice_in_dim(vectors[: 5 * d].reshape(5, d), me * n, n, 1)
    t = lax.axis_index("tensor")
    at = 5 * d
    vqk = vectors[at : at + groups * nqk].reshape(groups, tp, 2, HEAD_DIM)
    vv = vectors[at + groups * nqk : at + groups * (nqk + nv)].reshape(groups, tp, HEAD_DIM)
    vu = vectors[at + groups * (nqk + nv) :].reshape(parts, tp, FF_CHUNK)
    vqk = lax.dynamic_index_in_dim(vqk, t, 1, keepdims=False)
    grad_query_bias, grad_key_bias = vqk[:, 0].reshape(-1), vqk[:, 1].reshape(-1)
    grad_value_bias = lax.dynamic_index_in_dim(vv, t, 1, keepdims=False).reshape(-1)
    grad_up_bias = lax.dynamic_index_in_dim(vu, t, 1, keepdims=False).reshape(-1)
    return (
        block_out,
        grad_tokens,
        rows5[0:2],
        rows5[2:4],
        grad_w_query,
        grad_w_key,
        grad_w_value,
        grad_query_bias,
        grad_key_bias,
        grad_value_bias,
        grad_w_output.T,
        grad_w_up,
        grad_up_bias,
        grad_w_down.T,
        jnp.concatenate([rows5[4:5], rows5[4:5]]),
    )


def solution(mesh):
    rows = P(("dp", "tensor"), None)
    cols = P(None, ("dp", "tensor"))
    wide, tall, vec = P("dp", "tensor"), P("tensor", "dp"), P("tensor")
    return jax.shard_map(
        functools.partial(on_device, mesh.shape["dp"], mesh.shape["tensor"]),
        mesh=mesh,
        in_specs=(rows, cols, cols, wide, wide, wide, vec, vec, vec, tall, wide, vec, tall, cols, rows),
        out_specs=(
            rows, rows, cols, cols, wide, wide, wide, vec, vec, vec, tall, wide, vec, tall, cols,
        ),
        check_vma=False,
    )
```

```python
import functools

import jax
import jax.numpy as jnp
from jax import lax
from jax.experimental import pallas as pl
from jax.experimental.pallas import tpu as pltpu
from jax.sharding import PartitionSpec as P

HEAD_DIM = 64
ROT = 16
SEQ_LEN = 1024
EPSILON = 1e-05
PAIR = 2 * HEAD_DIM
Q_ROWS = 256
M_ROWS = 512
N_ROWS = 256
FF_CHUNK = 256
VMEM = 60 * 1024 * 1024
F32 = jnp.float32
BF16 = jnp.bfloat16


def dot_nn(a, b):
    return jnp.dot(a, b, preferred_element_type=F32)


def dot_nt(a, b):
    return lax.dot_general(a, b, (((1,), (1,)), ((), ())), preferred_element_type=F32)


def dot_tn(a, b):
    return lax.dot_general(a, b, (((0,), (0,)), ((), ())), preferred_element_type=F32)


def layer_stats(rows):
    center = rows - jnp.mean(rows, axis=1, keepdims=True)
    inverse = lax.rsqrt(jnp.mean(center * center, axis=1, keepdims=True) + EPSILON)
    return center * inverse, inverse


def norm_kernel(
    steps,
    me_ref,
    x_ref,
    dy_ref,
    gain_ref,
    bias_ref,
    a_ref,
    m_ref,
    at_ref,
    dyt_ref,
    mt_ref,
    dyp_ref,
    sum_ref,
):
    normed, _ = layer_stats(x_ref[...].astype(F32))
    a = normed * gain_ref[0:1] + bias_ref[0:1]
    m = normed * gain_ref[1:2] + bias_ref[1:2]
    dy = dy_ref[...].astype(F32)
    a_ref[...] = a.astype(BF16)
    m_ref[...] = m.astype(BF16)
    at_ref[...] = a.T.astype(BF16)
    mt = m.T.astype(BF16)
    dyt = dy.T.astype(BF16)
    dyt_ref[...] = dyt
    if steps is None:
        mt_ref[...] = mt
        dyp_ref[...] = dyt
    else:
        count = 1 << len(steps[0])
        own = mt.shape[0] // count
        for ref, value, order in ((mt_ref, mt, steps[0]), (dyp_ref, dyt, steps[1])):
            for owner in range(count):
                place = place_of(owner ^ me_ref[0], order)
                ref[pl.ds(pl.multiple_of(place * own, own), own), :] = value[
                    owner * own : (owner + 1) * own
                ]

    @pl.when(pl.program_id(0) == 0)
    def _():
        sum_ref[...] = jnp.zeros_like(sum_ref)

    sum_ref[...] += jnp.sum(dy, axis=0, keepdims=True)


def place_of(relative, order):
    place = 0
    for bit in order:
        place = place * 2 + ((relative // bit) % 2)
    return place


def rope_mix(u, tables, sign):
    c, s1, s2 = tables
    turned = pltpu.roll(u, PAIR - ROT // 2, 1) * s1 + pltpu.roll(u, ROT // 2, 1) * s2
    return u * c + turned if sign > 0 else u * c - turned


def attn_kernel(
    heads,
    *refs,
):
    w_refs = refs[:heads]
    attn_body(heads, w_refs, *refs[heads:])


def attn_body(
    heads,
    w_refs,
    x_ref,
    xt_ref,
    dy_ref,
    dyt_ref,
    bqk_ref,
    bv_ref,
    c_ref,
    s1_ref,
    s2_ref,
    o_s,
    dqk_s,
    dv_s,
    gw_ref,
    dbqk_ref,
    dbv_ref,
    qk_s,
    v_s,
    do_s,
    dq_s,
    dkt_s,
    dvt_s,
    oacc_s,
    s_s,
    dp_s,
    p_s,
    ds_s,
):
    nqk = heads * PAIR
    nv = heads * HEAD_DIM
    wqk = jnp.concatenate([w[:, :PAIR] for w in w_refs], axis=1)
    wv = jnp.concatenate([w[:, PAIR : PAIR + HEAD_DIM] for w in w_refs], axis=1)
    wo = jnp.concatenate([w[:, PAIR + HEAD_DIM :] for w in w_refs], axis=1)
    qk = dot_nn(x_ref[...], wqk) + bqk_ref[...]
    for t in range(heads):
        u = qk[:, t * PAIR : (t + 1) * PAIR]
        qk_s[t] = rope_mix(u, (c_ref[...], s1_ref[...], s2_ref[...]), 1).astype(BF16)
    v = (dot_nn(x_ref[...], wv) + bv_ref[...]).astype(BF16)
    do = dot_nn(dy_ref[...], wo).astype(BF16)
    for p in range(heads // 2):
        v_s[p] = v[:, p * PAIR : (p + 1) * PAIR]
        do_s[p] = do[:, p * PAIR : (p + 1) * PAIR]

    lane = lax.broadcasted_iota(jnp.int32, (1, PAIR), 1)
    low = lane < HEAD_DIM
    below = lax.broadcasted_iota(jnp.int32, (Q_ROWS, Q_ROWS), 0) >= lax.broadcasted_iota(
        jnp.int32, (Q_ROWS, Q_ROWS), 1
    )

    blocks = SEQ_LEN // Q_ROWS

    def one_pair(p, carry):
        v_p = v_s[p]
        do_p = do_s[p]
        for odd in range(2):
            t = p * 2 + odd
            mine = low if odd == 0 else lane >= HEAD_DIM
            qk_h = qk_s[t]
            kq = pltpu.roll(qk_h.astype(F32), HEAD_DIM, 1)
            kqt = kq.T.astype(BF16)
            kq = kq.astype(BF16)
            q_only = jnp.where(low, qk_h, jnp.zeros_like(qk_h))
            v_h = jnp.where(mine, v_p, jnp.zeros_like(v_p))
            do_h = jnp.where(mine, do_p, jnp.zeros_like(do_p))
            vt = v_h.T
            dot = do_h.T
            for j in range(blocks):
                c = slice(j * Q_ROWS, (j + 1) * Q_ROWS)
                s_s[odd, j * Q_ROWS :, c] = dot_nn(q_only[j * Q_ROWS :], kqt[:, c])
                dp_s[odd, j * Q_ROWS :, c] = dot_nn(do_h[j * Q_ROWS :], vt[:, c])
            for i in range(blocks):
                r = slice(i * Q_ROWS, (i + 1) * Q_ROWS)
                n = (i + 1) * Q_ROWS
                s = s_s[odd, r, :n]
                tail = jnp.where(below, s[:, n - Q_ROWS :], -1e30)
                s = tail if i == 0 else jnp.concatenate([s[:, : n - Q_ROWS], tail], axis=1)
                top = jnp.max(s, axis=1, keepdims=True)
                e = jnp.exp(s - top)
                total = jnp.sum(e, axis=1, keepdims=True)
                prob = e * (1.0 / total)
                p_s[odd, r, :n] = prob.astype(BF16)
                dp = dp_s[odd, r, :n]
                delta = jnp.sum(prob * dp, axis=1, keepdims=True)
                ds_s[odd, r, :n] = (prob * (dp - delta)).astype(BF16)
            for j in range(blocks):
                c = slice(j * Q_ROWS, (j + 1) * Q_ROWS)
                prob_low = p_s[odd, j * Q_ROWS :, c]
                ds = ds_s[odd, j * Q_ROWS :, c]
                o_part = dot_nn(prob_low, v_h[c])
                dq_part = dot_nn(ds, kq[c])
                if odd == 0 and j == 0:
                    oacc_s[...] = o_part
                else:
                    oacc_s[j * Q_ROWS :, :] += o_part
                if j == 0:
                    dq_s[odd] = dq_part
                else:
                    dq_s[odd, j * Q_ROWS :, :] += dq_part
                dkt_s[odd, :, c] = dot_nn(kqt[:, j * Q_ROWS :], ds)
                dv_part = dot_nn(dot[:, j * Q_ROWS :], prob_low)
                if odd == 0:
                    dvt_s[:, c] = dv_part
                else:
                    dvt_s[:, c] += dv_part
            dqk = jnp.where(low, dq_s[odd], dkt_s[odd].T)
            dqk = rope_mix(dqk, (c_ref[...], s1_ref[...], s2_ref[...]), -1)
            dqk_s[:, pl.ds(pl.multiple_of(t * PAIR, PAIR), PAIR)] = dqk.astype(BF16)
        at = pl.ds(pl.multiple_of(p * PAIR, PAIR), PAIR)
        dv_s[:, at] = dvt_s[...].T.astype(BF16)
        o_s[:, at] = oacc_s[...].astype(BF16)
        return carry

    lax.fori_loop(0, heads // 2, one_pair, 0)

    dqk_all = dqk_s[...]
    dv_all = dv_s[...]
    o_all = o_s[...]
    gqk = dot_nn(xt_ref[...], dqk_all)
    gv = dot_nn(xt_ref[...], dv_all)
    go = dot_nn(dyt_ref[...], o_all)
    for t in range(heads):
        at = 2 * PAIR * t
        h = slice(t * HEAD_DIM, (t + 1) * HEAD_DIM)
        gw_ref[:, at : at + PAIR] = gqk[:, t * PAIR : (t + 1) * PAIR].astype(BF16)
        gw_ref[:, at + PAIR : at + 2 * PAIR] = jnp.concatenate([gv[:, h], go[:, h]], axis=1).astype(BF16)
    dbqk_ref[...] = jnp.sum(dqk_all.astype(F32), axis=0, keepdims=True)
    dbv_ref[...] = jnp.sum(dv_all.astype(F32), axis=0, keepdims=True)


def mlp_kernel(
    heads, x_ref, xt_ref, dy_ref, dyt_ref, b_ref, *refs
):
    wu = jnp.concatenate([ref[...] for ref in refs[:heads]], axis=1)
    wd = jnp.concatenate([ref[...] for ref in refs[heads : 2 * heads]], axis=1)
    mlp_body(x_ref, xt_ref, dy_ref, dyt_ref, b_ref, wu, wd, *refs[2 * heads :])


def mlp_body(
    x_ref, xt_ref, dy_ref, dyt_ref, b_ref, wu, wd, y_ref, dx_ref, uk_ref, us_ref, dk_ref, ds_ref, db_ref, g_s, dh_s
):
    half = xt_ref.shape[0] // 2
    total = jnp.zeros(db_ref.shape, F32)
    for i in range(x_ref.shape[0] // M_ROWS):
        r = slice(i * M_ROWS, (i + 1) * M_ROWS)
        h = dot_nn(x_ref[r, :], wu) + b_ref[...]
        dg = dot_nn(dy_ref[r, :], wd)
        phi = 0.5 + 0.5 * lax.erf(h * (0.5**0.5))
        g = (h * phi).astype(BF16)
        slope = phi + h * (jnp.exp(h * h * -0.5) * 0.3989422804014327)
        dh = (dg * slope).astype(BF16)
        g_s[r, :] = g
        dh_s[r, :] = dh
        total += jnp.sum(dh.astype(F32), axis=0, keepdims=True)
        y = dot_nt(g, wd)
        dx = dot_nt(dh, wu)

        @pl.when(pl.program_id(0) == 0)
        def _():
            y_ref[r, :] = y
            dx_ref[r, :] = dx

        @pl.when(pl.program_id(0) != 0)
        def _():
            y_ref[r, :] += y
            dx_ref[r, :] += dx

    db_ref[...] = total
    g = g_s[...]
    dh = dh_s[...]
    us_ref[...] = dot_nn(xt_ref[half:, :], dh).astype(BF16)
    uk_ref[...] = dot_nn(xt_ref[:half, :], dh).astype(BF16)
    ds_ref[...] = dot_nn(dyt_ref[half:, :], g).astype(BF16)
    dk_ref[...] = dot_nn(dyt_ref[:half, :], g).astype(BF16)


def fold_kernel(uk_ref, ur_ref, dk_ref, dr_ref, *out_refs):
    half = uk_ref.shape[0] // 2
    for keep, got, outs in ((uk_ref, ur_ref, out_refs[:2]), (dk_ref, dr_ref, out_refs[2:])):
        outs[1][...] = (keep[half:, :].astype(F32) + got[half:, :].astype(F32)).astype(BF16)
        outs[0][...] = (keep[:half, :].astype(F32) + got[:half, :].astype(F32)).astype(BF16)


def split_kernel(uk_ref, ur_ref, dk_ref, dr_ref, *out_refs):
    size = len(out_refs)
    n = FF_CHUNK
    for p in range(uk_ref.shape[1] // (size * n)):
        for shift, out in enumerate(out_refs):
            at = slice((p * size + shift) * n, (p * size + shift + 1) * n)
            to = 2 * p * n
            out[:, to : to + n] = (uk_ref[:, at].astype(F32) + ur_ref[:, at].astype(F32)).astype(BF16)
            out[:, to + n : to + 2 * n] = (
                dk_ref[:, at].astype(F32) + dr_ref[:, at].astype(F32)
            ).astype(BF16)


def pack_kernel(groups, q_ref, k_ref, v_ref, o_ref, g_ref, b_ref, c_ref, long_ref, out_ref, vec_s):
    vec_s[...] = jnp.zeros_like(vec_s)
    for at, ref in ((0, g_ref), (2, b_ref), (4, c_ref)):
        vec_s[at : at + ref.shape[0], : ref.shape[1]] = ref[...].astype(F32)
    d = vec_s.shape[1]
    at = 0
    while at * d < long_ref.shape[1]:
        piece = long_ref[:, at * d : (at + 1) * d].astype(F32)
        vec_s[6 + at : 7 + at, : piece.shape[1]] = piece
        at += 1
    lines = vec_s.shape[0]
    out_ref[:lines, :] = vec_s[...].astype(BF16)
    turned = o_ref[...].astype(F32).T.astype(BF16)
    for j in range(groups):
        h = slice(j * HEAD_DIM, (j + 1) * HEAD_DIM)
        row = jnp.concatenate([q_ref[:, h], k_ref[:, h], v_ref[:, h], turned[:, h]], axis=1)
        out_ref[lines:, j * 2 * PAIR : (j + 1) * 2 * PAIR] = row


def cut_kernel(g_ref, *out_refs):
    size = len(out_refs)
    width = 2 * PAIR
    for s, out in enumerate(out_refs):
        for j in range(out.shape[1] // width):
            at = (j * size + s) * width
            out[:, j * width : (j + 1) * width] = g_ref[:, at : at + width]


def sum_refs(refs):
    total = refs[0][...].astype(F32)
    for ref in refs[1:]:
        total += ref[...].astype(F32)
    return total


def heads_grad_kernel(size, *refs):
    total = sum_refs(refs[:size])
    q_ref, k_ref, v_ref, o_ref = refs[size:]
    pick = lambda k: jnp.concatenate(
        [
            total[:, at + k * HEAD_DIM : at + (k + 1) * HEAD_DIM]
            for at in range(0, total.shape[1], 2 * PAIR)
        ],
        axis=1,
    )
    q_ref[...] = pick(0)
    k_ref[...] = pick(1)
    v_ref[...] = pick(2)
    o_ref[...] = pick(3).T


def mlp_grad_kernel(size, *refs):
    u_ref, d_ref = refs[-2:]
    n = FF_CHUNK
    p = 0
    for at in range(0, len(refs) - 2, size):
        total = sum_refs(refs[at : at + size])
        for start in range(0, total.shape[1], 2 * n):
            u_ref[:, p * n : (p + 1) * n] = total[:, start : start + n]
            d_ref[p * n : (p + 1) * n, :] = total[:, start + n : start + 2 * n].T
            p += 1


def vector_kernel(size, groups, parts, me_ref, *refs):
    ins = refs[:size]
    gain_ref, bias_ref, out_ref, q_ref, k_ref, v_ref, u_ref = refs[size:]
    d = ins[0].shape[1]
    n = gain_ref.shape[1]
    total = sum_refs(ins)[:8]
    at = lax.broadcasted_iota(jnp.int32, (d, n), 0) - lax.broadcasted_iota(jnp.int32, (d, n), 1)
    chosen = (at == me_ref[0] * n).astype(F32)
    mine = jnp.dot(total, chosen, precision=lax.Precision.HIGHEST, preferred_element_type=F32)
    gain_ref[...] = mine[0:2]
    bias_ref[...] = mine[2:4]
    out_ref[...] = jnp.concatenate([mine[4:5], mine[4:5]], axis=0)

    def block(start, index, width):
        value = None
        for s, ref in enumerate(ins):
            where = start + (index * size + (size - s) % size) * width
            part = ref[where // d : where // d + 1, where % d : where % d + width]
            value = part if value is None else value + part
        return value

    first = 5 * d
    for j in range(groups):
        h = slice(j * HEAD_DIM, (j + 1) * HEAD_DIM)
        both = block(first, j, PAIR)
        q_ref[:, h] = both[:, :HEAD_DIM]
        k_ref[:, h] = both[:, HEAD_DIM:]
        v_ref[:, h] = block(first + groups * size * PAIR, j, HEAD_DIM)
    first += groups * size * (PAIR + HEAD_DIM)
    for c in range(parts):
        u_ref[:, c * FF_CHUNK : (c + 1) * FF_CHUNK] = block(first, c, FF_CHUNK)


def heads_kernel(parts, heads, o_ref, dqk_ref, dv_ref, w_ref, y_ref, da_ref):
    y = da = None
    for j in range(parts):
        w = [w_ref[:, (t * parts + j) * 2 * PAIR : (t * parts + j + 1) * 2 * PAIR] for t in range(heads)]
        wqk = jnp.concatenate([u[:, :PAIR] for u in w], axis=1)
        wv = jnp.concatenate([u[:, PAIR : PAIR + HEAD_DIM] for u in w], axis=1)
        wo = jnp.concatenate([u[:, PAIR + HEAD_DIM :] for u in w], axis=1)
        nqk, nv = wqk.shape[1], wv.shape[1]
        y_j = dot_nt(o_ref[:, j * nv : (j + 1) * nv], wo)
        da_j = dot_nt(dqk_ref[:, j * nqk : (j + 1) * nqk], wqk)
        da_j += dot_nt(dv_ref[:, j * nv : (j + 1) * nv], wv)
        y = y_j if y is None else y + y_j
        da = da_j if da is None else da + da_j
    y_ref[...] = y
    da_ref[...] = da


def last_kernel(parts, lines, x_ref, dy_ref, ya_ref, da_ref, gain_ref, bias_ref, *refs):
    ym, dms = refs[:parts], refs[parts : 2 * parts]
    line_refs = refs[2 * parts : 2 * parts + lines]
    out_ref, dx_ref, sums_ref = refs[2 * parts + lines :]
    x = x_ref[...].astype(F32)
    normed, inverse = layer_stats(x)
    y = ya_ref[...] + bias_ref[0:1] + bias_ref[1:2]
    for part in ym:
        y += part[...]
    out_ref[...] = (x + y).astype(BF16)
    da = da_ref[...]
    dm = dms[0][...]
    for part in dms[1:]:
        dm += part[...]
    e = da * gain_ref[0:1] + dm * gain_ref[1:2]
    dx_ref[...] = dy_ref[...].astype(F32) + inverse * (
        e - jnp.mean(e, axis=1, keepdims=True) - normed * jnp.mean(e * normed, axis=1, keepdims=True)
    )

    @pl.when(pl.program_id(0) == 0)
    def _():
        sums_ref[...] = jnp.zeros_like(sums_ref)
        row = 4
        flat = jnp.concatenate([ref[...] for ref in line_refs], axis=1)
        d = sums_ref.shape[1]
        for at in range(0, flat.shape[1], d):
            sums_ref[row : row + 1, :] = flat[:, at : at + d]
            row += 1

    sums_ref[0:1] += jnp.sum(da * normed, axis=0, keepdims=True)
    sums_ref[1:2] += jnp.sum(dm * normed, axis=0, keepdims=True)
    sums_ref[2:3] += jnp.sum(da, axis=0, keepdims=True)
    sums_ref[3:4] += jnp.sum(dm, axis=0, keepdims=True)


def params():
    return pltpu.CompilerParams(
        dimension_semantics=("arbitrary",), vmem_limit_bytes=VMEM
    )


def whole(shape):
    return pl.BlockSpec(shape, lambda *_: (0,) * len(shape), pipeline_mode=pl.Buffered(1))


def whole_out(shape):
    return pl.BlockSpec(shape, lambda *_: (0,) * len(shape))


def waiting(kernel, count, where):
    if not count:
        return kernel

    def body(*refs):
        kernel(*refs[:where], *refs[where + count :])

    return body


def after(x, *deps):
    def body(x_ref, *refs):
        pass

    any_spec = pl.BlockSpec(memory_space=pl.ANY)
    return pl.pallas_call(
        body,
        in_specs=[any_spec] * (1 + len(deps)),
        out_specs=any_spec,
        out_shape=jax.ShapeDtypeStruct(x.shape, x.dtype),
        input_output_aliases={0: 0},
        name="after",
    )(x, *deps)


def any_specs(deps):
    return [pl.BlockSpec(memory_space=pl.ANY)] * len(deps)


def cost(*_):
    return pl.CostEstimate(flops=1024, bytes_accessed=1024, transcendentals=0)


def scalar_in():
    return pl.BlockSpec(memory_space=pltpu.SMEM)


def run_norm(me, tokens, cotangent, gains, biases, steps, deps=()):
    rows, d = tokens.shape
    by_row = pl.BlockSpec((N_ROWS, d), lambda i: (i, 0))
    by_col = pl.BlockSpec((d, N_ROWS), lambda i: (0, i))
    flat = jax.ShapeDtypeStruct((rows, d), BF16)
    turned = jax.ShapeDtypeStruct((d, rows), BF16)
    return pl.pallas_call(
        waiting(functools.partial(norm_kernel, steps), len(deps), 5),
        grid=(rows // N_ROWS,),
        in_specs=[scalar_in(), by_row, by_row, whole((2, d)), whole((2, d))] + any_specs(deps),
        out_specs=[by_row, by_row, by_col, by_col, by_col, by_col, whole_out((1, d))],
        out_shape=[flat, flat, turned, turned, turned, turned, jax.ShapeDtypeStruct((1, d), F32)],
        compiler_params=params(),
        cost_estimate=cost(40 * rows * d, 16 * rows * d),
        name="norm",
    )(me, tokens, cotangent, gains, biases, *deps)


def run_attn(x, xt, dy, dyt, w, bqk, bv, tables, heads, deps=()):
    rows, d = x.shape
    nqk, nv = heads * PAIR, heads * HEAD_DIM
    width = nqk + 2 * nv
    chunks = w.shape[1] // width
    member = lambda t: pl.BlockSpec((d, width // heads), lambda j, t=t: (0, t * chunks + j))
    per = lambda n: pl.BlockSpec((1, n), lambda j: (0, j))
    tall = lambda n: pl.BlockSpec((rows, n), lambda j: (0, j))
    half = (heads // 2, rows, PAIR)
    return pl.pallas_call(
        waiting(functools.partial(attn_kernel, heads), len(deps), 9 + heads),
        grid=(chunks,),
        in_specs=[member(t) for t in range(heads)]
        + [
            whole((rows, d)),
            whole((d, rows)),
            whole((rows, d)),
            whole((d, rows)),
            per(nqk),
            per(nv),
        ]
        + [whole((rows, PAIR))] * 3
        + any_specs(deps),
        out_specs=[
            tall(nv),
            tall(nqk),
            tall(nv),
            pl.BlockSpec((d, width), lambda j: (0, j)),
            per(nqk),
            per(nv),
        ],
        out_shape=[
            jax.ShapeDtypeStruct((rows, chunks * nv), BF16),
            jax.ShapeDtypeStruct((rows, chunks * nqk), BF16),
            jax.ShapeDtypeStruct((rows, chunks * nv), BF16),
            jax.ShapeDtypeStruct((d, chunks * width), BF16),
            jax.ShapeDtypeStruct((1, chunks * nqk), F32),
            jax.ShapeDtypeStruct((1, chunks * nv), F32),
        ],
        scratch_shapes=[
            pltpu.VMEM((heads, rows, PAIR), BF16),
            pltpu.VMEM(half, BF16),
            pltpu.VMEM(half, BF16),
            pltpu.VMEM((2, rows, PAIR), F32),
            pltpu.VMEM((2, PAIR, rows), F32),
            pltpu.VMEM((PAIR, rows), F32),
            pltpu.VMEM((rows, PAIR), F32),
            pltpu.VMEM((2, rows, rows), F32),
            pltpu.VMEM((2, rows, rows), F32),
            pltpu.VMEM((2, rows, rows), BF16),
            pltpu.VMEM((2, rows, rows), BF16),
        ],
        compiler_params=params(),
        cost_estimate=cost(
            4 * rows * d * chunks * width + 24 * chunks * heads * rows * rows * PAIR,
            20 * rows * d,
            chunks * heads * rows * rows,
        ),
        name="attention",
    )(*[w] * heads, x, xt, dy, dyt, bqk, bv, *tables, *deps)


def run_mlp(x, xt, dy, dyt, w, b, heads, first, count, deps=()):
    rows, d = x.shape
    n = FF_CHUNK
    parts = w.shape[1] // (2 * n * heads)
    width = heads * n
    half = d // 2
    by = lambda r, dt: jax.ShapeDtypeStruct((r, count * width), dt)
    member = lambda t, k: pl.BlockSpec((d, n), lambda p: (0, (t * parts + first + p) * 2 + k))
    tall = lambda r: pl.BlockSpec((r, width), lambda p: (0, p))
    return pl.pallas_call(
        waiting(functools.partial(mlp_kernel, heads), len(deps), 5 + 2 * heads),
        grid=(count,),
        in_specs=[
            whole((rows, d)),
            whole((d, rows)),
            whole((rows, d)),
            whole((d, rows)),
            pl.BlockSpec((1, width), lambda p: (0, first + p)),
        ]
        + [member(t, k) for k in range(2) for t in range(heads)]
        + any_specs(deps),
        out_specs=[whole_out((rows, d))] * 2 + [tall(half)] * 4 + [tall(1)],
        out_shape=[jax.ShapeDtypeStruct((rows, d), F32)] * 2 + [by(half, BF16)] * 4 + [by(1, F32)],
        scratch_shapes=[pltpu.VMEM((rows, width), BF16)] * 2,
        compiler_params=params(),
        cost_estimate=cost(),
        name="mlp",
    )(x, xt, dy, dyt, b, *[w] * (2 * heads), *deps)


def full_spec(x):
    return pl.BlockSpec(x.shape, lambda *_: (0,) * x.ndim)


def simple_call(kernel, name, ins, outs, deps=(), scratch=(), scalars=0):
    vmem = pl.BlockSpec(memory_space=pltpu.VMEM)
    return pl.pallas_call(
        waiting(kernel, len(deps), len(ins)),
        in_specs=[scalar_in()] * scalars + [vmem] * (len(ins) - scalars) + any_specs(deps),
        out_specs=[vmem] * len(outs),
        out_shape=[jax.ShapeDtypeStruct(shape, dt) for shape, dt in outs],
        scratch_shapes=scratch,
        compiler_params=pltpu.CompilerParams(vmem_limit_bytes=VMEM),
        cost_estimate=cost(),
        name=name,
    )(*ins, *deps)


def run_fold(arrays, deps=()):
    rows, n = arrays[0].shape
    return simple_call(fold_kernel, "fold", arrays, [((rows // 2, n), BF16)] * 4, deps)


def run_split(arrays, size, deps=()):
    rows, n = arrays[0].shape
    return simple_call(split_kernel, "split", arrays, [((rows, 2 * n // size), BF16)] * size, deps)


def run_heads(o, dqk, dv, w, heads, groups, deps=()):
    rows, d = o.shape[0], w.shape[0]
    tall = lambda n: pl.BlockSpec((M_ROWS, n), lambda i: (i, 0))
    return pl.pallas_call(
        waiting(functools.partial(heads_kernel, groups, heads), len(deps), 4),
        grid=(rows // M_ROWS,),
        in_specs=[tall(u.shape[1]) for u in (o, dqk, dv)] + [whole(w.shape)] + any_specs(deps),
        out_specs=[tall(d), tall(d)],
        out_shape=[jax.ShapeDtypeStruct((rows, d), F32)] * 2,
        compiler_params=params(),
        cost_estimate=cost(8 * rows * d * d, 20 * rows * d),
        name="heads",
    )(o, dqk, dv, w, *deps)


def run_last(tokens, dy, ya, da, gains, branch_bias, ym, dm, lines, deps):
    rows, d = tokens.shape
    by_row = pl.BlockSpec((N_ROWS, d), lambda i: (i, 0))
    parts = len(ym)
    count = -(-(4 + sum(u.shape[1] for u in lines) // d) // 8) * 8
    return pl.pallas_call(
        waiting(functools.partial(last_kernel, parts, len(lines)), len(deps), 6 + 2 * parts + len(lines)),
        grid=(rows // N_ROWS,),
        in_specs=[by_row] * 4
        + [whole((2, d))] * 2
        + [by_row] * (2 * parts)
        + [whole(u.shape) for u in lines]
        + any_specs(deps),
        out_specs=[by_row, by_row, whole_out((count, d))],
        out_shape=[
            jax.ShapeDtypeStruct((rows, d), BF16),
            jax.ShapeDtypeStruct((rows, d), F32),
            jax.ShapeDtypeStruct((count, d), F32),
        ],
        compiler_params=params(),
        cost_estimate=cost(60 * rows * d, 44 * rows * d),
        name="last",
    )(tokens, dy, ya, da, gains, branch_bias, *ym, *dm, *lines, *deps)


def ring(x, size, shift):
    return lax.ppermute(x, "tensor", [(i, (i - shift) % size) for i in range(size)])


def flip(x, size, bit):
    return lax.ppermute(x, "dp", [(i, i ^ bit) for i in range(size)])


def bits_of(size):
    return [1 << b for b in range(size.bit_length() - 1)]


def rotate_parts(parts, size):
    me = lax.axis_index("tensor")
    parts = jnp.stack(parts)
    return lax.dynamic_slice_in_dim(
        jnp.concatenate([parts, parts]), lax.rem(size - me, size), size, 0
    )


def gather_dp(x, size):
    me = lax.axis_index("dp")
    x = x[None]
    for bit in bits_of(size):
        other = flip(x, size, bit)
        mine_high = (me & bit) != 0
        x = jnp.concatenate([jnp.where(mine_high, other, x), jnp.where(mine_high, x, other)])
    return x


def send_blocks(blocks, size):
    return [blocks[0]] + [ring(blocks[s], size, size - s) for s in range(1, size)]


def rope_tables():
    positions = jnp.arange(SEQ_LEN, dtype=F32)
    frequency = 10000.0 ** (-2.0 * jnp.arange(ROT // 2, dtype=F32) / ROT)
    angles = positions[:, None] * frequency[None, :]
    cosine, sine = jnp.cos(angles), jnp.sin(angles)
    none = jnp.zeros_like(sine)
    rest = jnp.zeros((SEQ_LEN, HEAD_DIM - ROT), F32)
    c = jnp.concatenate([cosine, cosine, rest + 1.0], axis=1)
    s1 = jnp.concatenate([-sine, none, rest], axis=1)
    s2 = jnp.concatenate([none, sine, rest], axis=1)
    scale = HEAD_DIM**-0.5
    return [jnp.concatenate([u * scale, u], axis=1) for u in (c, s1, s2)]


def on_device(
    dp,
    tp,
    tokens,
    ln_gains,
    ln_biases,
    w_query,
    w_key,
    w_value,
    query_bias,
    key_bias,
    value_bias,
    w_output,
    w_up,
    up_bias,
    w_down,
    out_biases,
    cotangent,
):
    rows, d = tokens.shape
    own = w_query.shape[0]
    groups = w_query.shape[1] // HEAD_DIM
    hidden = w_up.shape[1]
    parts = hidden // FF_CHUNK
    nqk, nv = tp * PAIR, tp * HEAD_DIM
    a_width = nqk + 2 * nv
    f_width = tp * FF_CHUNK

    line = groups * 2 * PAIR
    flat = lambda u: u.reshape(1, -1)
    (pack,) = simple_call(
        functools.partial(pack_kernel, groups),
        "pack",
        [w_query, w_key, w_value, w_output, ln_gains, ln_biases, out_biases]
        + [flat(jnp.concatenate([query_bias, key_bias, value_bias, up_bias]))],
        [((16 + own, line), BF16)],
        scratch=[pltpu.VMEM((16, line), F32)],
    )
    packs = [pack] + [ring(pack, tp, s) for s in range(1, tp)]
    fa = jnp.concatenate([u[16:] for u in packs], axis=1)
    wf = jnp.stack([w.reshape(own, parts, FF_CHUNK) for w in (w_up, w_down.T)], axis=2)
    wf = after(wf.reshape(own, -1), fa)
    fa = lax.all_gather(fa, "dp", axis=0, tiled=True)
    n = ln_gains.shape[1]
    small = gather_dp(rotate_parts([u[:6, :n] for u in packs], tp), dp).astype(F32)
    small = small.transpose(2, 0, 1, 3).reshape(6, d)
    gains, biases, branch_bias = small[0:2], small[2:4], small[4:6]
    vec = jnp.stack([u[6:10] for u in packs]).astype(F32).reshape(tp, -1)
    hq = groups * HEAD_DIM
    by_head = lambda k: vec[:, k * hq : (k + 1) * hq].reshape(tp, groups, HEAD_DIM).transpose(1, 0, 2)
    bqk = flat(jnp.stack([by_head(0), by_head(1)], axis=2))
    bv = flat(by_head(2))
    bu = flat(vec[:, 3 * hq : 3 * hq + hidden].reshape(tp, parts, FF_CHUNK).transpose(1, 0, 2))
    ff_parts = [wf] + [ring(wf, tp, k) for k in range(1, tp)]

    tables = rope_tables()
    me_dp = lax.axis_index("dp").astype(jnp.int32).reshape(1)
    me_all = me_dp * tp + lax.axis_index("tensor").astype(jnp.int32)
    bits = bits_of(dp)
    steps = (bits, bits[:1] + bits[:0:-1]) if own % 16 == 0 and len(bits) == 3 else None
    attn_in, mlp_in, attn_t, dy_t, mlp_tp, dy_tp, dy_sum = run_norm(
        me_dp, tokens, cotangent, gains, biases, steps, [bqk, bv, *tables]
    )
    ff_parts[-1] = after(ff_parts[-1], attn_in)
    ff = ready = jnp.concatenate(ff_parts, axis=1)
    ff = lax.all_gather(ff, "dp", axis=0, tiled=True)
    o, dqk, dv, ga, dbqk, dbv = run_attn(
        attn_in, attn_t, cotangent, dy_t, fa, bqk, bv, tables, tp, [ready]
    )
    ga = after(ga, ff)
    ga = lax.psum_scatter(ga, "dp", scatter_dimension=0, tiled=True)
    dbu, ym, dm, pieces = [], [], [], []
    def mlp(first, count, deps):
        y_c, dm_c, uk, us, dk, ds, db = run_mlp(
            mlp_in, mlp_tp, cotangent, dy_tp, ff, bu, tp, first, count, deps
        )
        ym.append(y_c)
        dm.append(dm_c)
        dbu.append(db)
        return [uk, us, dk, ds]

    def heads():
        return run_heads(o, dqk, dv, fa, tp, groups, dm)

    def last(deps):
        lines = [dy_sum, dbqk, dbv] + dbu
        return run_last(tokens, cotangent, ya, da, gains, branch_bias, ym, dm, lines, deps)

    def cut(ga, deps):
        return simple_call(cut_kernel, "cut", [ga], [((own, line), BF16)] * tp, deps)

    early = parts - parts // 3
    if steps is None:
        for first, count in ((0, early), (early, parts - early)):
            uk, us, dk, ds = mlp(first, count, [dqk])
            if first == 0:
                ya, da = heads()
            both = []
            for keep, send in ((uk, us), (dk, ds)):
                u = jnp.concatenate([keep, send], axis=0)
                u = lax.psum_scatter(u, "dp", scatter_dimension=0, tiled=True)
                both.append(u.reshape(own, count, tp, FF_CHUNK))
            both = jnp.concatenate(both, axis=3)
            pieces.extend(send_blocks([both[:, :, s].reshape(own, -1) for s in range(tp)], tp))
        block_out, grad_tokens, vectors = last([])
        ga = cut(ga, [])
    else:
        def step(arrays, at, deps):
            uk, us, dk, ds = arrays
            ins = [uk, flip(us, dp, steps[0][at]), dk, flip(ds, dp, steps[1][at])]
            return run_fold(ins, deps) if at < 2 else run_split(ins, tp, deps)

        one = mlp(0, early, [dqk])
        ya, da = heads()
        one = step(one, 0, [da])
        two = mlp(early, parts - early, [one[1]])
        one = step(one, 1, [dm[1]])
        ga = cut(ga, [one[1]])
        two = step(two, 0, [ga[1]])
        one = step(one, 2, [two[1]])
        two = step(two, 1, [one[1]])
        block_out, grad_tokens, vectors = last([two[1]])
        two = step(two, 2, [vectors])
        pieces.extend(send_blocks(one, tp))
        pieces.extend(send_blocks(two, tp))
    for bit in bits_of(dp):
        vectors = vectors + flip(vectors, dp, bit)
    vectors = [vectors] + [ring(vectors, tp, s) for s in range(1, tp)]
    ga = send_blocks(ga, tp)

    wide, tall = ((own, groups * HEAD_DIM), F32), ((groups * HEAD_DIM, own), F32)
    grad_w_query, grad_w_key, grad_w_value, grad_w_output = simple_call(
        functools.partial(heads_grad_kernel, tp), "heads_grad", ga, [wide, wide, wide, tall]
    )
    grad_ln_gains, grad_ln_biases, grad_out_biases, gqb, gkb, gvb, gub = simple_call(
        functools.partial(vector_kernel, tp, groups, parts),
        "vectors",
        [me_all] + vectors,
        [((2, n), F32)] * 3 + [((1, groups * HEAD_DIM), F32)] * 3 + [((1, hidden), F32)],
        scalars=1,
    )
    grad_w_up, grad_w_down = simple_call(
        functools.partial(mlp_grad_kernel, tp),
        "mlp_grad",
        pieces,
        [((own, hidden), F32), ((hidden, own), F32)],
    )
    return (
        block_out,
        grad_tokens,
        grad_ln_gains,
        grad_ln_biases,
        grad_w_query,
        grad_w_key,
        grad_w_value,
        gqb.reshape(-1),
        gkb.reshape(-1),
        gvb.reshape(-1),
        grad_w_output,
        grad_w_up,
        gub.reshape(-1),
        grad_w_down,
        grad_out_biases,
    )


def solution(mesh):
    rows = P(("dp", "tensor"), None)
    cols = P(None, ("dp", "tensor"))
    wide, tall, vec = P("dp", "tensor"), P("tensor", "dp"), P("tensor")
    return jax.shard_map(
        functools.partial(on_device, mesh.shape["dp"], mesh.shape["tensor"]),
        mesh=mesh,
        in_specs=(rows, cols, cols, wide, wide, wide, vec, vec, vec, tall, wide, vec, tall, cols, rows),
        out_specs=(
            rows, rows, cols, cols, wide, wide, wide, vec, vec, vec, tall, wide, vec, tall, cols,
        ),
        check_vma=False,
    )
```

```python
import functools

import jax
import jax.numpy as jnp
from jax import lax
from jax.experimental import pallas as pl
from jax.experimental.pallas import tpu as pltpu
from jax.sharding import PartitionSpec as P

HEAD_DIM = 64
ROT = 16
SEQ_LEN = 1024
EPSILON = 1e-05
PAIR = 2 * HEAD_DIM
Q_ROWS = 256
M_ROWS = 512
N_ROWS = 256
FF_CHUNK = 256
VMEM = 60 * 1024 * 1024
F32 = jnp.float32
BF16 = jnp.bfloat16


def dot_nn(a, b):
    return jnp.dot(a, b, preferred_element_type=F32)


def dot_nt(a, b):
    return lax.dot_general(a, b, (((1,), (1,)), ((), ())), preferred_element_type=F32)


def dot_tn(a, b):
    return lax.dot_general(a, b, (((0,), (0,)), ((), ())), preferred_element_type=F32)


def layer_stats(rows):
    center = rows - jnp.mean(rows, axis=1, keepdims=True)
    inverse = lax.rsqrt(jnp.mean(center * center, axis=1, keepdims=True) + EPSILON)
    return center * inverse, inverse


def norm_kernel(
    steps,
    me_ref,
    x_ref,
    dy_ref,
    gain_ref,
    bias_ref,
    a_ref,
    m_ref,
    at_ref,
    dyt_ref,
    mt_ref,
    dyp_ref,
    sum_ref,
):
    normed, _ = layer_stats(x_ref[...].astype(F32))
    a = normed * gain_ref[0:1] + bias_ref[0:1]
    m = normed * gain_ref[1:2] + bias_ref[1:2]
    dy = dy_ref[...].astype(F32)
    a_ref[...] = a.astype(BF16)
    m_ref[...] = m.astype(BF16)
    mt = m.T.astype(BF16)
    dyt = dy.T.astype(BF16)
    at_ref[...] = a.T.astype(BF16)
    dyt_ref[...] = dyt
    if steps is None:
        mt_ref[...] = mt
        dyp_ref[...] = dyt
    else:
        count = 1 << len(steps[0])
        own = mt.shape[0] // count
        for ref, value, order in ((mt_ref, mt, steps[0]), (dyp_ref, dyt, steps[1])):
            for owner in range(count):
                place = place_of(owner ^ me_ref[0], order)
                ref[pl.ds(pl.multiple_of(place * own, own), own), :] = value[
                    owner * own : (owner + 1) * own
                ]

    @pl.when(pl.program_id(0) == 0)
    def _():
        sum_ref[...] = jnp.zeros_like(sum_ref)

    sum_ref[...] += jnp.sum(dy, axis=0, keepdims=True)


def place_of(relative, order):
    place = 0
    for bit in order:
        place = place * 2 + ((relative // bit) % 2)
    return place


def rope_mix(u, tables, sign):
    c, s1, s2 = tables
    turned = pltpu.roll(u, PAIR - ROT // 2, 1) * s1 + pltpu.roll(u, ROT // 2, 1) * s2
    return u * c + turned if sign > 0 else u * c - turned


def attn_kernel(
    heads,
    *refs,
):
    w_refs = refs[:heads]
    attn_body(heads, w_refs, *refs[heads:])


def attn_body(
    heads,
    w_refs,
    x_ref,
    xt_ref,
    dy_ref,
    dyt_ref,
    bqk_ref,
    bv_ref,
    c_ref,
    s1_ref,
    s2_ref,
    o_s,
    dqk_s,
    dv_s,
    gw_ref,
    dbqk_ref,
    dbv_ref,
    qk_s,
    v_s,
    do_s,
    dq_s,
    dkt_s,
    dvt_s,
    oacc_s,
    s_s,
    dp_s,
    p_s,
    ds_s,
):
    nqk = heads * PAIR
    nv = heads * HEAD_DIM
    wqk = jnp.concatenate([w[:, :PAIR] for w in w_refs], axis=1)
    wv = jnp.concatenate([w[:, PAIR : PAIR + HEAD_DIM] for w in w_refs], axis=1)
    wo = jnp.concatenate([w[:, PAIR + HEAD_DIM :] for w in w_refs], axis=1)
    qk = dot_nn(x_ref[...], wqk) + bqk_ref[...]
    for t in range(heads):
        u = qk[:, t * PAIR : (t + 1) * PAIR]
        qk_s[t] = rope_mix(u, (c_ref[...], s1_ref[...], s2_ref[...]), 1).astype(BF16)
    v = (dot_nn(x_ref[...], wv) + bv_ref[...]).astype(BF16)
    do = dot_nn(dy_ref[...], wo).astype(BF16)
    for p in range(heads // 2):
        v_s[p] = v[:, p * PAIR : (p + 1) * PAIR]
        do_s[p] = do[:, p * PAIR : (p + 1) * PAIR]

    lane = lax.broadcasted_iota(jnp.int32, (1, PAIR), 1)
    low = lane < HEAD_DIM
    below = lax.broadcasted_iota(jnp.int32, (Q_ROWS, Q_ROWS), 0) >= lax.broadcasted_iota(
        jnp.int32, (Q_ROWS, Q_ROWS), 1
    )

    blocks = SEQ_LEN // Q_ROWS

    def one_pair(p, carry):
        v_p = v_s[p]
        do_p = do_s[p]
        for odd in range(2):
            t = p * 2 + odd
            mine = low if odd == 0 else lane >= HEAD_DIM
            qk_h = qk_s[t]
            kq = pltpu.roll(qk_h.astype(F32), HEAD_DIM, 1)
            kqt = kq.T.astype(BF16)
            kq = kq.astype(BF16)
            q_only = jnp.where(low, qk_h, jnp.zeros_like(qk_h))
            v_h = jnp.where(mine, v_p, jnp.zeros_like(v_p))
            do_h = jnp.where(mine, do_p, jnp.zeros_like(do_p))
            vt = v_h.T
            dot = do_h.T
            for j in range(blocks):
                c = slice(j * Q_ROWS, (j + 1) * Q_ROWS)
                s_s[odd, j * Q_ROWS :, c] = dot_nn(q_only[j * Q_ROWS :], kqt[:, c])
                dp_s[odd, j * Q_ROWS :, c] = dot_nn(do_h[j * Q_ROWS :], vt[:, c])
            for i in range(blocks):
                r = slice(i * Q_ROWS, (i + 1) * Q_ROWS)
                n = (i + 1) * Q_ROWS
                s = s_s[odd, r, :n]
                tail = jnp.where(below, s[:, n - Q_ROWS :], -1e30)
                s = tail if i == 0 else jnp.concatenate([s[:, : n - Q_ROWS], tail], axis=1)
                top = jnp.max(s, axis=1, keepdims=True)
                e = jnp.exp(s - top)
                total = jnp.sum(e, axis=1, keepdims=True)
                prob = e * (1.0 / total)
                p_s[odd, r, :n] = prob.astype(BF16)
                dp = dp_s[odd, r, :n]
                delta = jnp.sum(prob * dp, axis=1, keepdims=True)
                ds_s[odd, r, :n] = (prob * (dp - delta)).astype(BF16)
            for j in range(blocks):
                c = slice(j * Q_ROWS, (j + 1) * Q_ROWS)
                prob_low = p_s[odd, j * Q_ROWS :, c]
                ds = ds_s[odd, j * Q_ROWS :, c]
                o_part = dot_nn(prob_low, v_h[c])
                dq_part = dot_nn(ds, kq[c])
                if odd == 0 and j == 0:
                    oacc_s[...] = o_part
                else:
                    oacc_s[j * Q_ROWS :, :] += o_part
                if j == 0:
                    dq_s[odd] = dq_part
                else:
                    dq_s[odd, j * Q_ROWS :, :] += dq_part
                dkt_s[odd, :, c] = dot_nn(kqt[:, j * Q_ROWS :], ds)
                dv_part = dot_nn(dot[:, j * Q_ROWS :], prob_low)
                if odd == 0:
                    dvt_s[:, c] = dv_part
                else:
                    dvt_s[:, c] += dv_part
            dqk = jnp.where(low, dq_s[odd], dkt_s[odd].T)
            dqk = rope_mix(dqk, (c_ref[...], s1_ref[...], s2_ref[...]), -1)
            dqk_s[:, pl.ds(pl.multiple_of(t * PAIR, PAIR), PAIR)] = dqk.astype(BF16)
        at = pl.ds(pl.multiple_of(p * PAIR, PAIR), PAIR)
        dv_s[:, at] = dvt_s[...].T.astype(BF16)
        o_s[:, at] = oacc_s[...].astype(BF16)
        return carry

    lax.fori_loop(0, heads // 2, one_pair, 0)

    dqk_all = dqk_s[...]
    dv_all = dv_s[...]
    o_all = o_s[...]
    gw_ref[:, :nqk] = dot_nn(xt_ref[...], dqk_all).astype(BF16)
    gv = dot_nn(xt_ref[...], dv_all)
    go = dot_nn(dyt_ref[...], o_all)
    for t in range(heads):
        h = slice(t * HEAD_DIM, (t + 1) * HEAD_DIM)
        gw_ref[:, nqk + t * PAIR : nqk + (t + 1) * PAIR] = jnp.concatenate(
            [gv[:, h], go[:, h]], axis=1
        ).astype(BF16)
    dbqk_ref[...] = jnp.sum(dqk_all.astype(F32), axis=0, keepdims=True)
    dbv_ref[...] = jnp.sum(dv_all.astype(F32), axis=0, keepdims=True)


def mlp_kernel(
    heads, x_ref, xt_ref, dy_ref, dyt_ref, b_ref, *refs
):
    wu = jnp.concatenate([ref[...] for ref in refs[:heads]], axis=1)
    wd = jnp.concatenate([ref[...] for ref in refs[heads : 2 * heads]], axis=1)
    mlp_body(x_ref, xt_ref, dy_ref, dyt_ref, b_ref, wu, wd, *refs[2 * heads :])


def mlp_body(
    x_ref, xt_ref, dy_ref, dyt_ref, b_ref, wu, wd, y_ref, dx_ref, uk_ref, us_ref, dk_ref, ds_ref, db_ref, g_s, dh_s, y_s, dx_s
):
    half = xt_ref.shape[0] // 2
    total = jnp.zeros(db_ref.shape, F32)
    for i in range(x_ref.shape[0] // M_ROWS):
        r = slice(i * M_ROWS, (i + 1) * M_ROWS)
        h = dot_nn(x_ref[r, :], wu) + b_ref[...]
        dg = dot_nn(dy_ref[r, :], wd)
        phi = 0.5 + 0.5 * lax.erf(h * (0.5**0.5))
        g = (h * phi).astype(BF16)
        slope = phi + h * (jnp.exp(h * h * -0.5) * 0.3989422804014327)
        dh = (dg * slope).astype(BF16)
        g_s[r, :] = g
        dh_s[r, :] = dh
        total += jnp.sum(dh.astype(F32), axis=0, keepdims=True)
        y = dot_nt(g, wd)
        dx = dot_nt(dh, wu)

        @pl.when(pl.program_id(0) == 0)
        def _():
            y_s[r, :] = y
            dx_s[r, :] = dx

        @pl.when(pl.program_id(0) != 0)
        def _():
            y_s[r, :] += y
            dx_s[r, :] += dx

    db_ref[...] = total
    g = g_s[...]
    dh = dh_s[...]
    us_ref[...] = dot_nn(xt_ref[half:, :], dh).astype(BF16)
    uk_ref[...] = dot_nn(xt_ref[:half, :], dh).astype(BF16)
    ds_ref[...] = dot_nn(dyt_ref[half:, :], g).astype(BF16)
    dk_ref[...] = dot_nn(dyt_ref[:half, :], g).astype(BF16)

    @pl.when(pl.program_id(0) == pl.num_programs(0) - 1)
    def _():
        y_ref[...] = y_s[...].astype(BF16)
        dx_ref[...] = dx_s[...].astype(BF16)


def add_low(a, b):
    return (a.astype(F32) + b.astype(F32)).astype(BF16)


def two_parts(lines):
    high = lines.astype(BF16)
    return high, (lines - high.astype(F32)).astype(BF16)


def lines_out(lines, width):
    rows = []
    for part in two_parts(lines):
        for at in range(0, lines.shape[1], width):
            piece = part[:, at : at + width]
            if piece.shape[1] < width:
                rest = jnp.zeros((piece.shape[0], width - piece.shape[1]), BF16)
                piece = jnp.concatenate([piece, rest], axis=1)
            rows.append(piece)
    return rows


def lines_in(rows, count, d):
    width = rows.shape[1]
    pieces = -(-d // width)
    total = None
    for part in range(2):
        own = [rows[(part * pieces + k) * count : (part * pieces + k + 1) * count] for k in range(pieces)]
        own = jnp.concatenate(own, axis=1)[:, :d].astype(F32)
        total = own if total is None else total + own
    return total


def lines_sum(lines, rows):
    high, low = two_parts(lines)
    return (high.astype(F32) + low.astype(F32)) + lines_in(rows, *lines.shape)


def fold_kernel(uk_ref, ur_ref, dk_ref, dr_ref, *refs):
    half = uk_ref.shape[0] // 2
    outs = refs[-5:] if len(refs) > 4 else refs
    for keep, got, out in ((uk_ref, ur_ref, outs[:2]), (dk_ref, dr_ref, outs[2:4])):
        out[1][:half, :] = add_low(keep[half:, :], got[half : 2 * half, :])
        out[0][...] = add_low(keep[:half, :], got[:half, :])
    if len(refs) > 4:
        if len(refs) == 7:
            lines = refs[0][...] + refs[1][...]
        else:
            lines = lines_sum(refs[0][...], ur_ref[2 * half :, :])
        outs[4][...] = lines
        at = half
        for rows in lines_out(lines, uk_ref.shape[1]):
            outs[1][at : at + rows.shape[0], :] = rows
            at += rows.shape[0]


def split_kernel(n, lined, uk_ref, ur_ref, dk_ref, dr_ref, *refs):
    out_refs = refs[1:] if lined else refs
    size = len(out_refs)
    own = uk_ref.shape[0]
    for p in range(uk_ref.shape[1] // (size * n)):
        for shift, out in enumerate(out_refs):
            at = slice((p * size + shift) * n, (p * size + shift + 1) * n)
            to = 2 * p * n
            out[:own, to : to + n] = add_low(uk_ref[:, at], ur_ref[:own, at])
            out[:own, to + n : to + 2 * n] = add_low(dk_ref[:, at], dr_ref[:, at])
    if lined:
        lines = lines_sum(refs[0][...], ur_ref[own:, :])
        at = own
        for rows in lines_out(lines, out_refs[0].shape[1]):
            for out in out_refs:
                out[at : at + rows.shape[0], :] = rows
            at += rows.shape[0]


def split_all_kernel(n, me_ref, uk_ref, ur_ref, dk_ref, dr_ref, out_ref):
    size = out_ref.shape[0]
    for p in range(uk_ref.shape[1] // (size * n)):
        for shift in range(size):
            owner = lax.rem(me_ref[0] + shift, size)
            at = slice((p * size + shift) * n, (p * size + shift + 1) * n)
            to = 2 * p * n
            out_ref[owner, :, to : to + n] = add_low(uk_ref[:, at], ur_ref[:, at])
            out_ref[owner, :, to + n : to + 2 * n] = add_low(dk_ref[:, at], dr_ref[:, at])


def pack_kernel(groups, q_ref, k_ref, v_ref, o_ref, g_ref, b_ref, c_ref, long_ref, out_ref, vec_s):
    vec_s[...] = jnp.zeros_like(vec_s)
    for at, ref in ((0, g_ref), (2, b_ref), (4, c_ref)):
        vec_s[at : at + ref.shape[0], : ref.shape[1]] = ref[...].astype(F32)
    d = vec_s.shape[1]
    at = 0
    while at * d < long_ref.shape[1]:
        piece = long_ref[:, at * d : (at + 1) * d].astype(F32)
        vec_s[6 + at : 7 + at, : piece.shape[1]] = piece
        at += 1
    lines = vec_s.shape[0]
    out_ref[:lines, :] = vec_s[...].astype(BF16)
    turned = o_ref[...].astype(F32).T.astype(BF16)
    for j in range(groups):
        h = slice(j * HEAD_DIM, (j + 1) * HEAD_DIM)
        row = jnp.concatenate([q_ref[:, h], k_ref[:, h], v_ref[:, h], turned[:, h]], axis=1)
        out_ref[lines:, j * 2 * PAIR : (j + 1) * 2 * PAIR] = row


def cut_kernel(me_ref, g_ref, out_ref):
    size = out_ref.shape[0]
    for s in range(size):
        owner = lax.rem(me_ref[0] + s, size)
        for k in range(out_ref.shape[2] // PAIR):
            at = (k * size + s) * PAIR
            out_ref[owner, :, k * PAIR : (k + 1) * PAIR] = g_ref[:, at : at + PAIR]


def sum_refs(refs, rows):
    total = refs[0][:rows, :].astype(F32)
    for ref in refs[1:]:
        total += ref[:rows, :].astype(F32)
    return total


def heads_grad_kernel(size, *refs):
    total = sum_refs(refs[:size], refs[0].shape[0])
    q_ref, k_ref, v_ref, o_ref = refs[size:]
    pick = lambda k: jnp.concatenate(
        [
            total[:, at + k * HEAD_DIM : at + (k + 1) * HEAD_DIM]
            for at in range(0, total.shape[1], 2 * PAIR)
        ],
        axis=1,
    )
    q_ref[...] = pick(0)
    k_ref[...] = pick(1)
    v_ref[...] = pick(2)
    o_ref[...] = pick(3).T


def mlp_grad_kernel(sizes, *refs):
    u_ref, d_ref = refs[-2:]
    n = FF_CHUNK
    p = at = 0
    for size in sizes:
        total = sum_refs(refs[at : at + size], u_ref.shape[0])
        at += size
        for start in range(0, total.shape[1], 2 * n):
            u_ref[:, p * n : (p + 1) * n] = total[:, start : start + n]
            d_ref[:, p * n : (p + 1) * n] = total[:, start + n : start + 2 * n]
            p += 1


def vector_kernel(size, groups, parts, own, count, d, me_ref, *refs):
    ins = refs[:size]
    gain_ref, bias_ref, out_ref, q_ref, k_ref, v_ref, u_ref = refs[size:]
    n = gain_ref.shape[1]
    if ins[0].dtype == BF16:
        ins = [lines_in(ref[own:, :], count, d) for ref in ins]
    else:
        ins = [ref[...] for ref in ins]
    total = ins[0][:8]
    for lines in ins[1:]:
        total += lines[:8]
    at = lax.broadcasted_iota(jnp.int32, (d, n), 0) - lax.broadcasted_iota(jnp.int32, (d, n), 1)
    chosen = (at == me_ref[0] * n).astype(F32)
    mine = jnp.dot(total, chosen, precision=lax.Precision.HIGHEST, preferred_element_type=F32)
    gain_ref[...] = mine[0:2]
    bias_ref[...] = mine[2:4]
    out_ref[...] = jnp.concatenate([mine[4:5], mine[4:5]], axis=0)

    def block(start, index, width):
        value = None
        for s, ref in enumerate(ins):
            where = start + (index * size + s) * width
            part = ref[where // d : where // d + 1, where % d : where % d + width]
            value = part if value is None else value + part
        return value

    first = 5 * d
    for j in range(groups):
        h = slice(j * HEAD_DIM, (j + 1) * HEAD_DIM)
        both = block(first, j, PAIR)
        q_ref[:, h] = both[:, :HEAD_DIM]
        k_ref[:, h] = both[:, HEAD_DIM:]
        v_ref[:, h] = block(first + groups * size * PAIR, j, HEAD_DIM)
    first += groups * size * (PAIR + HEAD_DIM)
    for c in range(parts):
        u_ref[:, c * FF_CHUNK : (c + 1) * FF_CHUNK] = block(first, c, FF_CHUNK)


def member_columns(w_ref, parts, heads, j, low, high):
    at = lambda t: (t * parts + j) * 2 * PAIR
    return jnp.concatenate([w_ref[:, at(t) + low : at(t) + high] for t in range(heads)], axis=1)


def heads_out_kernel(parts, heads, o_ref, w_ref, y_ref):
    y = None
    for j in range(parts):
        wo = member_columns(w_ref, parts, heads, j, PAIR + HEAD_DIM, 2 * PAIR)
        nv = wo.shape[1]
        y_j = dot_nt(o_ref[:, j * nv : (j + 1) * nv], wo)
        y = y_j if y is None else y + y_j
    y_ref[...] = y.astype(BF16)


def heads_back_kernel(parts, heads, dqk_ref, dv_ref, w_ref, da_ref):
    da = None
    for j in range(parts):
        wqk = member_columns(w_ref, parts, heads, j, 0, PAIR)
        wv = member_columns(w_ref, parts, heads, j, PAIR, PAIR + HEAD_DIM)
        nqk, nv = wqk.shape[1], wv.shape[1]
        da_j = dot_nt(dqk_ref[:, j * nqk : (j + 1) * nqk], wqk)
        da_j += dot_nt(dv_ref[:, j * nv : (j + 1) * nv], wv)
        da = da_j if da is None else da + da_j
    da_ref[...] = da.astype(BF16)


def last_kernel(parts, lines, x_ref, dy_ref, ya_ref, da_ref, gain_ref, bias_ref, *refs):
    ym, dms = refs[:parts], refs[parts : 2 * parts]
    line_refs = refs[2 * parts : 2 * parts + lines]
    out_ref, dx_ref, sums_ref = refs[2 * parts + lines :]
    x = x_ref[...].astype(F32)
    normed, inverse = layer_stats(x)
    y = ya_ref[...].astype(F32) + bias_ref[0:1] + bias_ref[1:2]
    for part in ym:
        y += part[...].astype(F32)
    out_ref[...] = (x + y).astype(BF16)
    da = da_ref[...].astype(F32)
    dm = dms[0][...].astype(F32)
    for part in dms[1:]:
        dm += part[...].astype(F32)
    e = da * gain_ref[0:1] + dm * gain_ref[1:2]
    dx_ref[...] = dy_ref[...].astype(F32) + inverse * (
        e - jnp.mean(e, axis=1, keepdims=True) - normed * jnp.mean(e * normed, axis=1, keepdims=True)
    )

    @pl.when(pl.program_id(0) == 0)
    def _():
        sums_ref[...] = jnp.zeros_like(sums_ref)
        row = 4
        flat = jnp.concatenate([ref[...] for ref in line_refs], axis=1)
        d = sums_ref.shape[1]
        for at in range(0, flat.shape[1], d):
            sums_ref[row : row + 1, :] = flat[:, at : at + d]
            row += 1

    sums_ref[0:1] += jnp.sum(da * normed, axis=0, keepdims=True)
    sums_ref[1:2] += jnp.sum(dm * normed, axis=0, keepdims=True)
    sums_ref[2:3] += jnp.sum(da, axis=0, keepdims=True)
    sums_ref[3:4] += jnp.sum(dm, axis=0, keepdims=True)


def params():
    return pltpu.CompilerParams(
        dimension_semantics=("arbitrary",), vmem_limit_bytes=VMEM
    )


def whole(shape):
    return pl.BlockSpec(shape, lambda *_: (0,) * len(shape), pipeline_mode=pl.Buffered(1))


def whole_out(shape):
    return pl.BlockSpec(shape, lambda *_: (0,) * len(shape))


def waiting(kernel, count, where):
    if not count:
        return kernel

    def body(*refs):
        kernel(*refs[:where], *refs[where + count :])

    return body


def after(x, *deps):
    def body(x_ref, *refs):
        pass

    any_spec = pl.BlockSpec(memory_space=pl.ANY)
    return pl.pallas_call(
        body,
        in_specs=[any_spec] * (1 + len(deps)),
        out_specs=any_spec,
        out_shape=jax.ShapeDtypeStruct(x.shape, x.dtype),
        input_output_aliases={0: 0},
        name="after",
    )(x, *deps)


def any_specs(deps):
    return [pl.BlockSpec(memory_space=pl.ANY)] * len(deps)


def cost(*_):
    return pl.CostEstimate(flops=1024, bytes_accessed=1024, transcendentals=0)


def scalar_in():
    return pl.BlockSpec(memory_space=pltpu.SMEM)


def run_norm(me, tokens, cotangent, gains, biases, steps, deps=()):
    rows, d = tokens.shape
    by_row = pl.BlockSpec((N_ROWS, d), lambda i: (i, 0))
    by_col = pl.BlockSpec((d, N_ROWS), lambda i: (0, i))
    flat = jax.ShapeDtypeStruct((rows, d), BF16)
    turned = jax.ShapeDtypeStruct((d, rows), BF16)
    return pl.pallas_call(
        waiting(functools.partial(norm_kernel, steps), len(deps), 5),
        grid=(rows // N_ROWS,),
        in_specs=[scalar_in(), by_row, by_row, whole((2, d)), whole((2, d))] + any_specs(deps),
        out_specs=[by_row, by_row, by_col, by_col, by_col, by_col, whole_out((1, d))],
        out_shape=[flat, flat, turned, turned, turned, turned, jax.ShapeDtypeStruct((1, d), F32)],
        compiler_params=params(),
        cost_estimate=cost(40 * rows * d, 16 * rows * d),
        name="norm",
    )(me, tokens, cotangent, gains, biases, *deps)


def run_attn(x, xt, dy, dyt, w, bqk, bv, tables, heads, deps=()):
    rows, d = x.shape
    nqk, nv = heads * PAIR, heads * HEAD_DIM
    width = nqk + 2 * nv
    chunks = w.shape[1] // width
    member = lambda t: pl.BlockSpec((d, width // heads), lambda j, t=t: (0, t * chunks + j))
    per = lambda n: pl.BlockSpec((1, n), lambda j: (0, j))
    tall = lambda n: pl.BlockSpec((rows, n), lambda j: (0, j))
    half = (heads // 2, rows, PAIR)
    return pl.pallas_call(
        waiting(functools.partial(attn_kernel, heads), len(deps), 9 + heads),
        grid=(chunks,),
        in_specs=[member(t) for t in range(heads)]
        + [
            whole((rows, d)),
            whole((d, rows)),
            whole((rows, d)),
            whole((d, rows)),
            per(nqk),
            per(nv),
        ]
        + [whole((rows, PAIR))] * 3
        + any_specs(deps),
        out_specs=[
            tall(nv),
            tall(nqk),
            tall(nv),
            pl.BlockSpec((d, width), lambda j: (0, j)),
            per(nqk),
            per(nv),
        ],
        out_shape=[
            jax.ShapeDtypeStruct((rows, chunks * nv), BF16),
            jax.ShapeDtypeStruct((rows, chunks * nqk), BF16),
            jax.ShapeDtypeStruct((rows, chunks * nv), BF16),
            jax.ShapeDtypeStruct((d, chunks * width), BF16),
            jax.ShapeDtypeStruct((1, chunks * nqk), F32),
            jax.ShapeDtypeStruct((1, chunks * nv), F32),
        ],
        scratch_shapes=[
            pltpu.VMEM((heads, rows, PAIR), BF16),
            pltpu.VMEM(half, BF16),
            pltpu.VMEM(half, BF16),
            pltpu.VMEM((2, rows, PAIR), F32),
            pltpu.VMEM((2, PAIR, rows), F32),
            pltpu.VMEM((PAIR, rows), F32),
            pltpu.VMEM((rows, PAIR), F32),
            pltpu.VMEM((2, rows, rows), F32),
            pltpu.VMEM((2, rows, rows), F32),
            pltpu.VMEM((2, rows, rows), BF16),
            pltpu.VMEM((2, rows, rows), BF16),
        ],
        compiler_params=params(),
        cost_estimate=cost(
            4 * rows * d * chunks * width + 24 * chunks * heads * rows * rows * PAIR,
            20 * rows * d,
            chunks * heads * rows * rows,
        ),
        name="attention",
    )(*[w] * heads, x, xt, dy, dyt, bqk, bv, *tables, *deps)


def run_mlp(x, xt, dy, dyt, w, b, heads, first, count, deps=()):
    rows, d = x.shape
    n = FF_CHUNK
    parts = w.shape[1] // (2 * n * heads)
    width = heads * n
    half = d // 2
    by = lambda r, dt: jax.ShapeDtypeStruct((r, count * width), dt)
    member = lambda t, k: pl.BlockSpec((d, n), lambda p: (0, (t * parts + first + p) * 2 + k))
    tall = lambda r: pl.BlockSpec((r, width), lambda p: (0, p))
    return pl.pallas_call(
        waiting(functools.partial(mlp_kernel, heads), len(deps), 5 + 2 * heads),
        grid=(count,),
        in_specs=[
            whole((rows, d)),
            whole((d, rows)),
            whole((rows, d)),
            whole((d, rows)),
            pl.BlockSpec((1, width), lambda p: (0, first + p)),
        ]
        + [member(t, k) for k in range(2) for t in range(heads)]
        + any_specs(deps),
        out_specs=[whole_out((rows, d))] * 2 + [tall(half)] * 4 + [tall(1)],
        out_shape=[jax.ShapeDtypeStruct((rows, d), BF16)] * 2 + [by(half, BF16)] * 4 + [by(1, F32)],
        scratch_shapes=[pltpu.VMEM((rows, width), BF16)] * 2 + [pltpu.VMEM((rows, d), F32)] * 2,
        compiler_params=params(),
        cost_estimate=cost(),
        name="mlp",
    )(x, xt, dy, dyt, b, *[w] * (2 * heads), *deps)


def full_spec(x):
    return pl.BlockSpec(x.shape, lambda *_: (0,) * x.ndim)


def simple_call(kernel, name, ins, outs, deps=(), scratch=(), scalars=0):
    vmem = pl.BlockSpec(memory_space=pltpu.VMEM)
    return pl.pallas_call(
        waiting(kernel, len(deps), len(ins)),
        in_specs=[scalar_in()] * scalars + [vmem] * (len(ins) - scalars) + any_specs(deps),
        out_specs=[vmem] * len(outs),
        out_shape=[jax.ShapeDtypeStruct(shape, dt) for shape, dt in outs],
        scratch_shapes=scratch,
        compiler_params=pltpu.CompilerParams(vmem_limit_bytes=VMEM),
        cost_estimate=cost(),
        name=name,
    )(*ins, *deps)


def run_fold(arrays, deps=()):
    rows, n = arrays[0].shape
    half = rows // 2
    outs = [((half, n), BF16)] * 4
    if len(arrays) > 4:
        count, d = arrays[4].shape
        outs[1] = ((half + 2 * count * -(-d // n), n), BF16)
        outs.append(((count, d), F32))
    return simple_call(fold_kernel, "fold", arrays, outs, deps)


def run_split(arrays, size, n, deps=()):
    rows, width = arrays[0].shape
    width = 2 * width // size
    lined = len(arrays) > 4
    if lined:
        count, d = arrays[4].shape
        rows += 2 * count * -(-d // width)
    outs = [((rows, width), BF16)] * size
    return simple_call(functools.partial(split_kernel, n, lined), "split", arrays, outs, deps)


def run_heads(kernel, name, acts, w, heads, groups, deps=()):
    rows, d = acts[0].shape[0], w.shape[0]
    tall = lambda n: pl.BlockSpec((M_ROWS, n), lambda i: (i, 0))
    return pl.pallas_call(
        waiting(functools.partial(kernel, groups, heads), len(deps), len(acts) + 1),
        grid=(rows // M_ROWS,),
        in_specs=[tall(u.shape[1]) for u in acts] + [whole(w.shape)] + any_specs(deps),
        out_specs=tall(d),
        out_shape=jax.ShapeDtypeStruct((rows, d), BF16),
        compiler_params=params(),
        cost_estimate=cost(),
        name=name,
    )(*acts, w, *deps)


def run_last(tokens, dy, ya, da, gains, branch_bias, ym, dm, lines, deps):
    rows, d = tokens.shape
    by_row = pl.BlockSpec((N_ROWS, d), lambda i: (i, 0))
    parts = len(ym)
    count = -(-(4 + sum(u.shape[1] for u in lines) // d) // 8) * 8
    return pl.pallas_call(
        waiting(functools.partial(last_kernel, parts, len(lines)), len(deps), 6 + 2 * parts + len(lines)),
        grid=(rows // N_ROWS,),
        in_specs=[by_row] * 4
        + [whole((2, d))] * 2
        + [by_row] * (2 * parts)
        + [whole(u.shape) for u in lines]
        + any_specs(deps),
        out_specs=[by_row, by_row, whole_out((count, d))],
        out_shape=[
            jax.ShapeDtypeStruct((rows, d), BF16),
            jax.ShapeDtypeStruct((rows, d), F32),
            jax.ShapeDtypeStruct((count, d), F32),
        ],
        compiler_params=params(),
        cost_estimate=cost(60 * rows * d, 44 * rows * d),
        name="last",
    )(tokens, dy, ya, da, gains, branch_bias, *ym, *dm, *lines, *deps)


def ring(x, size, shift):
    return lax.ppermute(x, "tensor", [(i, (i - shift) % size) for i in range(size)])


def flip(x, size, bit):
    return lax.ppermute(x, "dp", [(i, i ^ bit) for i in range(size)])


def bits_of(size):
    return [1 << b for b in range(size.bit_length() - 1)]


def rotate_parts(parts, size):
    me = lax.axis_index("tensor")
    parts = jnp.stack(parts)
    return lax.dynamic_slice_in_dim(
        jnp.concatenate([parts, parts]), lax.rem(size - me, size), size, 0
    )


def gather_dp(x, size):
    me = lax.axis_index("dp")
    x = x[None]
    for bit in bits_of(size):
        other = flip(x, size, bit)
        mine_high = (me & bit) != 0
        x = jnp.concatenate([jnp.where(mine_high, other, x), jnp.where(mine_high, x, other)])
    return x


def send_blocks(blocks, size):
    return [blocks[0]] + [ring(blocks[s], size, size - s) for s in range(1, size)]


def rope_tables():
    positions = jnp.arange(SEQ_LEN, dtype=F32)
    frequency = 10000.0 ** (-2.0 * jnp.arange(ROT // 2, dtype=F32) / ROT)
    angles = positions[:, None] * frequency[None, :]
    cosine, sine = jnp.cos(angles), jnp.sin(angles)
    none = jnp.zeros_like(sine)
    rest = jnp.zeros((SEQ_LEN, HEAD_DIM - ROT), F32)
    c = jnp.concatenate([cosine, cosine, rest + 1.0], axis=1)
    s1 = jnp.concatenate([-sine, none, rest], axis=1)
    s2 = jnp.concatenate([none, sine, rest], axis=1)
    scale = HEAD_DIM**-0.5
    return [jnp.concatenate([u * scale, u], axis=1) for u in (c, s1, s2)]


def on_device(
    dp,
    tp,
    tokens,
    ln_gains,
    ln_biases,
    w_query,
    w_key,
    w_value,
    query_bias,
    key_bias,
    value_bias,
    w_output,
    w_up,
    up_bias,
    w_down,
    out_biases,
    cotangent,
):
    rows, d = tokens.shape
    own = w_query.shape[0]
    groups = w_query.shape[1] // HEAD_DIM
    hidden = w_up.shape[1]
    parts = hidden // FF_CHUNK
    nqk, nv = tp * PAIR, tp * HEAD_DIM
    a_width = nqk + 2 * nv
    f_width = tp * FF_CHUNK

    line = groups * 2 * PAIR
    flat = lambda u: u.reshape(1, -1)
    (pack,) = simple_call(
        functools.partial(pack_kernel, groups),
        "pack",
        [w_query, w_key, w_value, w_output, ln_gains, ln_biases, out_biases]
        + [flat(jnp.concatenate([query_bias, key_bias, value_bias, up_bias]))],
        [((16 + own, line), BF16)],
        scratch=[pltpu.VMEM((16, line), F32)],
    )
    packs = [pack] + [ring(pack, tp, s) for s in range(1, tp)]
    fa = jnp.concatenate([u[16:] for u in packs], axis=1)
    wf = jnp.stack([w.reshape(own, parts, FF_CHUNK) for w in (w_up, w_down.T)], axis=2)
    wf = after(wf.reshape(own, -1), fa)
    fa = lax.all_gather(fa, "dp", axis=0, tiled=True)
    n = ln_gains.shape[1]
    small = gather_dp(rotate_parts([u[:6, :n] for u in packs], tp), dp).astype(F32)
    small = small.transpose(2, 0, 1, 3).reshape(6, d)
    gains, biases, branch_bias = small[0:2], small[2:4], small[4:6]
    vec = jnp.stack([u[6:10] for u in packs]).astype(F32).reshape(tp, -1)
    hq = groups * HEAD_DIM
    by_head = lambda k: vec[:, k * hq : (k + 1) * hq].reshape(tp, groups, HEAD_DIM).transpose(1, 0, 2)
    bqk = flat(jnp.stack([by_head(0), by_head(1)], axis=2))
    bv = flat(by_head(2))
    bu = flat(vec[:, 3 * hq : 3 * hq + hidden].reshape(tp, parts, FF_CHUNK).transpose(1, 0, 2))
    ff_parts = [wf] + [ring(wf, tp, k) for k in range(1, tp)]

    tables = rope_tables()
    me_dp = lax.axis_index("dp").astype(jnp.int32).reshape(1)
    me_tp = lax.axis_index("tensor").astype(jnp.int32).reshape(1)
    me_all = me_dp * tp + me_tp
    bits = bits_of(dp)
    steps = (bits, bits[:1] + bits[:0:-1]) if own % 16 == 0 and len(bits) == 3 else None
    attn_in, mlp_in, attn_t, dy_t, mlp_tp, dy_tp, dy_sum = run_norm(
        me_dp, tokens, cotangent, gains, biases, steps, [bqk, bv, *tables]
    )
    ff_parts[-1] = after(ff_parts[-1], attn_in)
    ready = jnp.concatenate(ff_parts, axis=1)
    ff = lax.all_gather(ready, "dp", axis=0, tiled=True)
    o, dqk, dv, ga, dbqk, dbv = run_attn(
        attn_in, attn_t, cotangent, dy_t, fa, bqk, bv, tables, tp, [ready]
    )
    early = parts - parts // 3
    dbu, ym, dm = [], [], []
    def mlp(first, count, deps):
        y_c, dm_c, uk, us, dk, ds, db = run_mlp(
            mlp_in, mlp_tp, cotangent, dy_tp, ff, bu, tp, first, count, deps
        )
        ym.append(y_c)
        dm.append(dm_c)
        dbu.append(db)
        return [uk, us, dk, ds]

    da = run_heads(heads_back_kernel, "heads_back", [dqk, dv], fa, tp, groups)

    ga = lax.psum_scatter(after(ga, ff, da), "dp", scatter_dimension=0, tiled=True)

    def heads_out(deps):
        return run_heads(heads_out_kernel, "heads_out", [o], fa, tp, groups, deps)

    def cut(u, deps):
        outs = [((tp, own, line), BF16)]
        (u,) = simple_call(cut_kernel, "cut", [me_tp, u], outs, deps, scalars=1)
        return u

    def last(ya, deps):
        lines = [dy_sum, dbqk, dbv] + dbu
        return run_last(tokens, cotangent, ya, da, gains, branch_bias, ym, dm, lines, deps)

    def finish_heads(blocks):
        total = lax.psum_scatter(blocks, "tensor", scatter_dimension=0, tiled=True)[0]
        wide, tall = ((own, groups * HEAD_DIM), F32), ((groups * HEAD_DIM, own), F32)
        kernel = functools.partial(heads_grad_kernel, 1)
        return simple_call(kernel, "heads_grad", [total], [wide, wide, wide, tall])

    if steps is None:

        def reduce(arrays, n):
            uk, us, dk, ds = arrays
            both = []
            for keep, send in ((uk, us), (dk, ds)):
                u = jnp.concatenate([keep, send], axis=0)
                u = lax.psum_scatter(u, "dp", scatter_dimension=0, tiled=True)
                both.append(u.reshape(own, -1, tp, n))
            both = jnp.concatenate(both, axis=3)
            return send_blocks([both[:, :, s].reshape(own, -1) for s in range(tp)], tp)

        head_grads = finish_heads(cut(ga, []))
        one = reduce(mlp(0, early, []), FF_CHUNK)
        two = reduce(mlp(early, parts - early, []), FF_CHUNK)
        block_out, grad_tokens, vectors = last(heads_out([]), [])
        for bit in bits_of(dp):
            vectors = vectors + flip(vectors, dp, bit)
        lines_shape = vectors.shape
        vectors = [vectors] + [ring(vectors, tp, tp - s) for s in range(1, tp)]
    else:
        def step(arrays, at, deps, n=FF_CHUNK):
            uk, us, dk, ds, *lines = arrays
            ins = [uk, flip(us, dp, steps[0][at]), dk, flip(ds, dp, steps[1][at]), *lines]
            if lines and at == 0:
                ins.append(flip(lines[0], dp, steps[0][0]))
            if at < 2:
                return run_fold(ins, deps)
            if lines:
                return run_split(ins, tp, n, deps)
            outs = [((tp, own, 2 * uk.shape[1] // tp), BF16)]
            kernel = functools.partial(split_all_kernel, n)
            return simple_call(kernel, "split_all", [me_tp, *ins], outs, deps, scalars=1)[0]

        hold = lambda arrays, *deps: [after(u, *deps) if k in (1, 3) else u for k, u in enumerate(arrays)]
        one = mlp(0, early, [da])
        ya = heads_out([dm[0]])
        one = step(one, 0, [ya])
        two = mlp(early, parts - early, [one[1]])
        ga = cut(ga, [dm[1]])
        one = step(one, 1, [ga])
        two = hold(two, one[1])
        block_out, grad_tokens, lines = last(ya, [one[1]])
        lines_shape = lines.shape
        one = step(one, 2, [lines])
        two = step([*two, lines], 0, [one])
        two = step(two, 1, [two[1]])
        two = step(two, 2, [two[1]])
        head_grads = finish_heads(ga)
        one = [lax.psum_scatter(one, "tensor", scatter_dimension=0, tiled=True)[0]]
        two = vectors = send_blocks(two, tp)
    pieces = [*one, *two]

    grad_w_query, grad_w_key, grad_w_value, grad_w_output = head_grads
    grad_ln_gains, grad_ln_biases, grad_out_biases, gqb, gkb, gvb, gub = simple_call(
        functools.partial(vector_kernel, tp, groups, parts, own, *lines_shape),
        "vectors",
        [me_all] + vectors,
        [((2, n), F32)] * 3 + [((1, groups * HEAD_DIM), F32)] * 3 + [((1, hidden), F32)],
        scalars=1,
    )
    grad_w_up, grad_w_down = simple_call(
        functools.partial(mlp_grad_kernel, (len(one), len(two))),
        "mlp_grad",
        pieces,
        [((own, hidden), F32)] * 2,
    )
    return (
        block_out,
        grad_tokens,
        grad_ln_gains,
        grad_ln_biases,
        grad_w_query,
        grad_w_key,
        grad_w_value,
        gqb.reshape(-1),
        gkb.reshape(-1),
        gvb.reshape(-1),
        grad_w_output,
        grad_w_up,
        gub.reshape(-1),
        grad_w_down.T,
        grad_out_biases,
    )


def solution(mesh):
    rows = P(("dp", "tensor"), None)
    cols = P(None, ("dp", "tensor"))
    wide, tall, vec = P("dp", "tensor"), P("tensor", "dp"), P("tensor")
    return jax.shard_map(
        functools.partial(on_device, mesh.shape["dp"], mesh.shape["tensor"]),
        mesh=mesh,
        in_specs=(rows, cols, cols, wide, wide, wide, vec, vec, vec, tall, wide, vec, tall, cols, rows),
        out_specs=(
            rows, rows, cols, cols, wide, wide, wide, vec, vec, vec, tall, wide, vec, tall, cols,
        ),
        check_vma=False,
    )
```

```python
import functools

import jax
import jax.numpy as jnp
from jax import lax
from jax.experimental import pallas as pl
from jax.experimental.pallas import tpu as pltpu
from jax.sharding import PartitionSpec as P

HEAD_DIM = 64
ROT = 16
SEQ_LEN = 1024
EPSILON = 1e-05
PAIR = 2 * HEAD_DIM
Q_ROWS = 256
M_ROWS = 512
N_ROWS = 256
FF_CHUNK = 256
VMEM = 60 * 1024 * 1024
F32 = jnp.float32
BF16 = jnp.bfloat16


def dot_nn(a, b):
    return jnp.dot(a, b, preferred_element_type=F32)


def dot_nt(a, b):
    return lax.dot_general(a, b, (((1,), (1,)), ((), ())), preferred_element_type=F32)


def dot_tn(a, b):
    return lax.dot_general(a, b, (((0,), (0,)), ((), ())), preferred_element_type=F32)


def layer_stats(rows):
    center = rows - jnp.mean(rows, axis=1, keepdims=True)
    inverse = lax.rsqrt(jnp.mean(center * center, axis=1, keepdims=True) + EPSILON)
    return center * inverse, inverse


def norm_kernel(
    steps,
    me_ref,
    x_ref,
    dy_ref,
    gain_ref,
    bias_ref,
    a_ref,
    m_ref,
    at_ref,
    dyt_ref,
    mt_ref,
    dyp_ref,
    sum_ref,
):
    normed, _ = layer_stats(x_ref[...].astype(F32))
    a = normed * gain_ref[0:1] + bias_ref[0:1]
    m = normed * gain_ref[1:2] + bias_ref[1:2]
    dy = dy_ref[...].astype(F32)
    a_ref[...] = a.astype(BF16)
    m_ref[...] = m.astype(BF16)
    mt = m.T.astype(BF16)
    dyt = dy.T.astype(BF16)
    at_ref[...] = a.T.astype(BF16)
    dyt_ref[...] = dyt
    if steps is None:
        mt_ref[...] = mt
        dyp_ref[...] = dyt
    else:
        count = 1 << len(steps[0])
        own = mt.shape[0] // count
        for ref, value, order in ((mt_ref, mt, steps[0]), (dyp_ref, dyt, steps[1])):
            for owner in range(count):
                place = place_of(owner ^ me_ref[0], order)
                ref[pl.ds(pl.multiple_of(place * own, own), own), :] = value[
                    owner * own : (owner + 1) * own
                ]

    @pl.when(pl.program_id(0) == 0)
    def _():
        sum_ref[...] = jnp.zeros_like(sum_ref)

    sum_ref[...] += jnp.sum(dy, axis=0, keepdims=True)


def place_of(relative, order):
    place = 0
    for bit in order:
        place = place * 2 + ((relative // bit) % 2)
    return place


def rope_mix(u, tables, sign):
    c, s1, s2 = tables
    turned = pltpu.roll(u, PAIR - ROT // 2, 1) * s1 + pltpu.roll(u, ROT // 2, 1) * s2
    return u * c + turned if sign > 0 else u * c - turned


def attn_kernel(
    heads,
    *refs,
):
    w_refs = refs[:heads]
    attn_body(heads, w_refs, *refs[heads:])


def attn_body(
    heads,
    w_refs,
    x_ref,
    xt_ref,
    dy_ref,
    dyt_ref,
    bqk_ref,
    bv_ref,
    c_ref,
    s1_ref,
    s2_ref,
    o_s,
    dqk_s,
    dv_s,
    gw_ref,
    dbqk_ref,
    dbv_ref,
    qk_s,
    v_s,
    do_s,
    dq_s,
    dkt_s,
    dvt_s,
    oacc_s,
    s_s,
    dp_s,
    p_s,
    ds_s,
):
    nqk = heads * PAIR
    nv = heads * HEAD_DIM
    wqk = jnp.concatenate([w[:, :PAIR] for w in w_refs], axis=1)
    wv = jnp.concatenate([w[:, PAIR : PAIR + HEAD_DIM] for w in w_refs], axis=1)
    wo = jnp.concatenate([w[:, PAIR + HEAD_DIM :] for w in w_refs], axis=1)
    qk = dot_nn(x_ref[...], wqk) + bqk_ref[...]
    for t in range(heads):
        u = qk[:, t * PAIR : (t + 1) * PAIR]
        qk_s[t] = rope_mix(u, (c_ref[...], s1_ref[...], s2_ref[...]), 1).astype(BF16)
    v = (dot_nn(x_ref[...], wv) + bv_ref[...]).astype(BF16)
    do = dot_nn(dy_ref[...], wo).astype(BF16)
    for p in range(heads // 2):
        v_s[p] = v[:, p * PAIR : (p + 1) * PAIR]
        do_s[p] = do[:, p * PAIR : (p + 1) * PAIR]

    lane = lax.broadcasted_iota(jnp.int32, (1, PAIR), 1)
    low = lane < HEAD_DIM
    below = lax.broadcasted_iota(jnp.int32, (Q_ROWS, Q_ROWS), 0) >= lax.broadcasted_iota(
        jnp.int32, (Q_ROWS, Q_ROWS), 1
    )

    blocks = SEQ_LEN // Q_ROWS

    def one_pair(p, carry):
        v_p = v_s[p]
        do_p = do_s[p]
        for odd in range(2):
            t = p * 2 + odd
            mine = low if odd == 0 else lane >= HEAD_DIM
            qk_h = qk_s[t]
            kq = pltpu.roll(qk_h.astype(F32), HEAD_DIM, 1)
            kqt = kq.T.astype(BF16)
            kq = kq.astype(BF16)
            q_only = jnp.where(low, qk_h, jnp.zeros_like(qk_h))
            v_h = jnp.where(mine, v_p, jnp.zeros_like(v_p))
            do_h = jnp.where(mine, do_p, jnp.zeros_like(do_p))
            vt = v_h.T
            dot = do_h.T
            for j in range(blocks):
                c = slice(j * Q_ROWS, (j + 1) * Q_ROWS)
                s_s[odd, j * Q_ROWS :, c] = dot_nn(q_only[j * Q_ROWS :], kqt[:, c])
                dp_s[odd, j * Q_ROWS :, c] = dot_nn(do_h[j * Q_ROWS :], vt[:, c])
            for i in range(blocks):
                r = slice(i * Q_ROWS, (i + 1) * Q_ROWS)
                n = (i + 1) * Q_ROWS
                s = s_s[odd, r, :n]
                tail = jnp.where(below, s[:, n - Q_ROWS :], -1e30)
                s = tail if i == 0 else jnp.concatenate([s[:, : n - Q_ROWS], tail], axis=1)
                top = jnp.max(s, axis=1, keepdims=True)
                e = jnp.exp(s - top)
                total = jnp.sum(e, axis=1, keepdims=True)
                prob = e * (1.0 / total)
                p_s[odd, r, :n] = prob.astype(BF16)
                dp = dp_s[odd, r, :n]
                delta = jnp.sum(prob * dp, axis=1, keepdims=True)
                ds_s[odd, r, :n] = (prob * (dp - delta)).astype(BF16)
            for j in range(blocks):
                c = slice(j * Q_ROWS, (j + 1) * Q_ROWS)
                prob_low = p_s[odd, j * Q_ROWS :, c]
                ds = ds_s[odd, j * Q_ROWS :, c]
                o_part = dot_nn(prob_low, v_h[c])
                dq_part = dot_nn(ds, kq[c])
                if odd == 0 and j == 0:
                    oacc_s[...] = o_part
                else:
                    oacc_s[j * Q_ROWS :, :] += o_part
                if j == 0:
                    dq_s[odd] = dq_part
                else:
                    dq_s[odd, j * Q_ROWS :, :] += dq_part
                dkt_s[odd, :, c] = dot_nn(kqt[:, j * Q_ROWS :], ds)
                dv_part = dot_nn(dot[:, j * Q_ROWS :], prob_low)
                if odd == 0:
                    dvt_s[:, c] = dv_part
                else:
                    dvt_s[:, c] += dv_part
            dqk = jnp.where(low, dq_s[odd], dkt_s[odd].T)
            dqk = rope_mix(dqk, (c_ref[...], s1_ref[...], s2_ref[...]), -1)
            dqk_s[:, pl.ds(pl.multiple_of(t * PAIR, PAIR), PAIR)] = dqk.astype(BF16)
        at = pl.ds(pl.multiple_of(p * PAIR, PAIR), PAIR)
        dv_s[:, at] = dvt_s[...].T.astype(BF16)
        o_s[:, at] = oacc_s[...].astype(BF16)
        return carry

    lax.fori_loop(0, heads // 2, one_pair, 0)

    dqk_all = dqk_s[...]
    dv_all = dv_s[...]
    o_all = o_s[...]
    gw_ref[:, :nqk] = dot_nn(xt_ref[...], dqk_all).astype(BF16)
    gv = dot_nn(xt_ref[...], dv_all)
    go = dot_nn(dyt_ref[...], o_all)
    for t in range(heads):
        h = slice(t * HEAD_DIM, (t + 1) * HEAD_DIM)
        gw_ref[:, nqk + t * PAIR : nqk + (t + 1) * PAIR] = jnp.concatenate(
            [gv[:, h], go[:, h]], axis=1
        ).astype(BF16)
    dbqk_ref[...] = jnp.sum(dqk_all.astype(F32), axis=0, keepdims=True)
    dbv_ref[...] = jnp.sum(dv_all.astype(F32), axis=0, keepdims=True)


def mlp_kernel(
    heads, x_ref, xt_ref, dy_ref, dyt_ref, b_ref, *refs
):
    wu = jnp.concatenate([ref[...] for ref in refs[:heads]], axis=1)
    wd = jnp.concatenate([ref[...] for ref in refs[heads : 2 * heads]], axis=1)
    mlp_body(x_ref, xt_ref, dy_ref, dyt_ref, b_ref, wu, wd, *refs[2 * heads :])


def mlp_body(
    x_ref, xt_ref, dy_ref, dyt_ref, b_ref, wu, wd, y_ref, dx_ref, uk_ref, us_ref, dk_ref, ds_ref, db_ref, g_s, dh_s, y_s, dx_s
):
    half = xt_ref.shape[0] // 2
    total = jnp.zeros(db_ref.shape, F32)
    for i in range(x_ref.shape[0] // M_ROWS):
        r = slice(i * M_ROWS, (i + 1) * M_ROWS)
        h = dot_nn(x_ref[r, :], wu) + b_ref[...]
        dg = dot_nn(dy_ref[r, :], wd)
        phi = 0.5 + 0.5 * lax.erf(h * (0.5**0.5))
        g = (h * phi).astype(BF16)
        slope = phi + h * (jnp.exp(h * h * -0.5) * 0.3989422804014327)
        dh = (dg * slope).astype(BF16)
        g_s[r, :] = g
        dh_s[r, :] = dh
        total += jnp.sum(dh.astype(F32), axis=0, keepdims=True)
        y = dot_nt(g, wd)
        dx = dot_nt(dh, wu)

        @pl.when(pl.program_id(0) == 0)
        def _():
            y_s[r, :] = y
            dx_s[r, :] = dx

        @pl.when(pl.program_id(0) != 0)
        def _():
            y_s[r, :] += y
            dx_s[r, :] += dx

    db_ref[...] = total
    g = g_s[...]
    dh = dh_s[...]
    us_ref[...] = dot_nn(xt_ref[half:, :], dh).astype(BF16)
    uk_ref[...] = dot_nn(xt_ref[:half, :], dh).astype(BF16)
    ds_ref[...] = dot_nn(dyt_ref[half:, :], g).astype(BF16)
    dk_ref[...] = dot_nn(dyt_ref[:half, :], g).astype(BF16)

    @pl.when(pl.program_id(0) == pl.num_programs(0) - 1)
    def _():
        y_ref[...] = y_s[...].astype(BF16)
        dx_ref[...] = dx_s[...].astype(BF16)


def add_low(a, b):
    return (a.astype(F32) + b.astype(F32)).astype(BF16)


def two_parts(lines):
    high = lines.astype(BF16)
    return high, (lines - high.astype(F32)).astype(BF16)


def lines_out(lines, width):
    rows = []
    for part in two_parts(lines):
        for at in range(0, lines.shape[1], width):
            piece = part[:, at : at + width]
            if piece.shape[1] < width:
                rest = jnp.zeros((piece.shape[0], width - piece.shape[1]), BF16)
                piece = jnp.concatenate([piece, rest], axis=1)
            rows.append(piece)
    return rows


def lines_in(rows, count, d):
    width = rows.shape[1]
    pieces = -(-d // width)
    total = None
    for part in range(2):
        own = [rows[(part * pieces + k) * count : (part * pieces + k + 1) * count] for k in range(pieces)]
        own = jnp.concatenate(own, axis=1)[:, :d].astype(F32)
        total = own if total is None else total + own
    return total


def lines_sum(lines, rows):
    high, low = two_parts(lines)
    return (high.astype(F32) + low.astype(F32)) + lines_in(rows, *lines.shape)


def fold_kernel(uk_ref, ur_ref, dk_ref, dr_ref, *refs):
    half = uk_ref.shape[0] // 2
    outs = refs[-5:] if len(refs) > 4 else refs
    for keep, got, out in ((uk_ref, ur_ref, outs[:2]), (dk_ref, dr_ref, outs[2:4])):
        out[1][:half, :] = add_low(keep[half:, :], got[half : 2 * half, :])
        out[0][...] = add_low(keep[:half, :], got[:half, :])
    if len(refs) > 4:
        if len(refs) == 7:
            lines = refs[0][...] + refs[1][...]
        else:
            lines = lines_sum(refs[0][...], ur_ref[2 * half :, :])
        outs[4][...] = lines
        at = half
        for rows in lines_out(lines, uk_ref.shape[1]):
            outs[1][at : at + rows.shape[0], :] = rows
            at += rows.shape[0]


def split_kernel(n, lined, uk_ref, ur_ref, dk_ref, dr_ref, *refs):
    out_refs = refs[1:] if lined else refs
    size = len(out_refs)
    own = uk_ref.shape[0]
    for p in range(uk_ref.shape[1] // (size * n)):
        for shift, out in enumerate(out_refs):
            at = slice((p * size + shift) * n, (p * size + shift + 1) * n)
            to = 2 * p * n
            out[:own, to : to + n] = add_low(uk_ref[:, at], ur_ref[:own, at])
            out[:own, to + n : to + 2 * n] = add_low(dk_ref[:, at], dr_ref[:, at])
    if lined:
        lines = lines_sum(refs[0][...], ur_ref[own:, :])
        at = own
        for rows in lines_out(lines, out_refs[0].shape[1]):
            for out in out_refs:
                out[at : at + rows.shape[0], :] = rows
            at += rows.shape[0]


def split_all_kernel(n, me_ref, uk_ref, ur_ref, dk_ref, dr_ref, out_ref):
    size = out_ref.shape[0]
    for p in range(uk_ref.shape[1] // (size * n)):
        for shift in range(size):
            owner = lax.rem(me_ref[0] + shift, size)
            at = slice((p * size + shift) * n, (p * size + shift + 1) * n)
            to = 2 * p * n
            out_ref[owner, :, to : to + n] = add_low(uk_ref[:, at], ur_ref[:, at])
            out_ref[owner, :, to + n : to + 2 * n] = add_low(dk_ref[:, at], dr_ref[:, at])


def pack_kernel(groups, q_ref, k_ref, v_ref, o_ref, g_ref, b_ref, c_ref, long_ref, out_ref, vec_s):
    vec_s[...] = jnp.zeros_like(vec_s)
    for at, ref in ((0, g_ref), (2, b_ref), (4, c_ref)):
        vec_s[at : at + ref.shape[0], : ref.shape[1]] = ref[...].astype(F32)
    d = vec_s.shape[1]
    at = 0
    while at * d < long_ref.shape[1]:
        piece = long_ref[:, at * d : (at + 1) * d].astype(F32)
        vec_s[6 + at : 7 + at, : piece.shape[1]] = piece
        at += 1
    lines = vec_s.shape[0]
    out_ref[:lines, :] = vec_s[...].astype(BF16)
    turned = o_ref[...].astype(F32).T.astype(BF16)
    for j in range(groups):
        h = slice(j * HEAD_DIM, (j + 1) * HEAD_DIM)
        row = jnp.concatenate([q_ref[:, h], k_ref[:, h], v_ref[:, h], turned[:, h]], axis=1)
        out_ref[lines:, j * 2 * PAIR : (j + 1) * 2 * PAIR] = row


def cut_kernel(me_ref, g_ref, out_ref):
    size = out_ref.shape[0]
    for s in range(size):
        owner = lax.rem(me_ref[0] + s, size)
        for k in range(out_ref.shape[2] // PAIR):
            at = (k * size + s) * PAIR
            out_ref[owner, :, k * PAIR : (k + 1) * PAIR] = g_ref[:, at : at + PAIR]


def sum_refs(refs, rows):
    total = refs[0][:rows, :].astype(F32)
    for ref in refs[1:]:
        total += ref[:rows, :].astype(F32)
    return total


def heads_grad_kernel(size, *refs):
    total = sum_refs(refs[:size], refs[0].shape[0])
    q_ref, k_ref, v_ref, o_ref = refs[size:]
    pick = lambda k: jnp.concatenate(
        [
            total[:, at + k * HEAD_DIM : at + (k + 1) * HEAD_DIM]
            for at in range(0, total.shape[1], 2 * PAIR)
        ],
        axis=1,
    )
    q_ref[...] = pick(0)
    k_ref[...] = pick(1)
    v_ref[...] = pick(2)
    o_ref[...] = pick(3).T


def mlp_grad_kernel(sizes, *refs):
    u_ref, d_ref = refs[-2:]
    n = FF_CHUNK
    p = at = 0
    for size in sizes:
        total = sum_refs(refs[at : at + size], u_ref.shape[0])
        at += size
        for start in range(0, total.shape[1], 2 * n):
            u_ref[:, p * n : (p + 1) * n] = total[:, start : start + n]
            d_ref[:, p * n : (p + 1) * n] = total[:, start + n : start + 2 * n]
            p += 1


def vector_kernel(size, groups, parts, own, count, d, me_ref, *refs):
    ins = refs[:size]
    gain_ref, bias_ref, out_ref, q_ref, k_ref, v_ref, u_ref = refs[size:]
    n = gain_ref.shape[1]
    if ins[0].dtype == BF16:
        ins = [lines_in(ref[own:, :], count, d) for ref in ins]
    else:
        ins = [ref[...] for ref in ins]
    total = ins[0][:8]
    for lines in ins[1:]:
        total += lines[:8]
    at = lax.broadcasted_iota(jnp.int32, (d, n), 0) - lax.broadcasted_iota(jnp.int32, (d, n), 1)
    chosen = (at == me_ref[0] * n).astype(F32)
    mine = jnp.dot(total, chosen, precision=lax.Precision.HIGHEST, preferred_element_type=F32)
    gain_ref[...] = mine[0:2]
    bias_ref[...] = mine[2:4]
    out_ref[...] = jnp.concatenate([mine[4:5], mine[4:5]], axis=0)

    def block(start, index, width):
        value = None
        for s, ref in enumerate(ins):
            where = start + (index * size + s) * width
            part = ref[where // d : where // d + 1, where % d : where % d + width]
            value = part if value is None else value + part
        return value

    first = 5 * d
    for j in range(groups):
        h = slice(j * HEAD_DIM, (j + 1) * HEAD_DIM)
        both = block(first, j, PAIR)
        q_ref[:, h] = both[:, :HEAD_DIM]
        k_ref[:, h] = both[:, HEAD_DIM:]
        v_ref[:, h] = block(first + groups * size * PAIR, j, HEAD_DIM)
    first += groups * size * (PAIR + HEAD_DIM)
    for c in range(parts):
        u_ref[:, c * FF_CHUNK : (c + 1) * FF_CHUNK] = block(first, c, FF_CHUNK)


def member_columns(w_ref, parts, heads, j, low, high):
    at = lambda t: (t * parts + j) * 2 * PAIR
    return jnp.concatenate([w_ref[:, at(t) + low : at(t) + high] for t in range(heads)], axis=1)


def heads_out_kernel(parts, heads, o_ref, w_ref, y_ref):
    y = None
    for j in range(parts):
        wo = member_columns(w_ref, parts, heads, j, PAIR + HEAD_DIM, 2 * PAIR)
        nv = wo.shape[1]
        y_j = dot_nt(o_ref[:, j * nv : (j + 1) * nv], wo)
        y = y_j if y is None else y + y_j
    y_ref[...] = y.astype(BF16)


def heads_back_kernel(parts, heads, dqk_ref, dv_ref, w_ref, da_ref):
    da = None
    for j in range(parts):
        wqk = member_columns(w_ref, parts, heads, j, 0, PAIR)
        wv = member_columns(w_ref, parts, heads, j, PAIR, PAIR + HEAD_DIM)
        nqk, nv = wqk.shape[1], wv.shape[1]
        da_j = dot_nt(dqk_ref[:, j * nqk : (j + 1) * nqk], wqk)
        da_j += dot_nt(dv_ref[:, j * nv : (j + 1) * nv], wv)
        da = da_j if da is None else da + da_j
    da_ref[...] = da.astype(BF16)


def last_kernel(parts, lines, x_ref, dy_ref, ya_ref, da_ref, gain_ref, bias_ref, *refs):
    ym, dms = refs[:parts], refs[parts : 2 * parts]
    line_refs = refs[2 * parts : 2 * parts + lines]
    out_ref, dx_ref, sums_ref = refs[2 * parts + lines :]
    x = x_ref[...].astype(F32)
    normed, inverse = layer_stats(x)
    y = ya_ref[...].astype(F32) + bias_ref[0:1] + bias_ref[1:2]
    for part in ym:
        y += part[...].astype(F32)
    out_ref[...] = (x + y).astype(BF16)
    da = da_ref[...].astype(F32)
    dm = dms[0][...].astype(F32)
    for part in dms[1:]:
        dm += part[...].astype(F32)
    e = da * gain_ref[0:1] + dm * gain_ref[1:2]
    dx_ref[...] = dy_ref[...].astype(F32) + inverse * (
        e - jnp.mean(e, axis=1, keepdims=True) - normed * jnp.mean(e * normed, axis=1, keepdims=True)
    )

    @pl.when(pl.program_id(0) == 0)
    def _():
        sums_ref[...] = jnp.zeros_like(sums_ref)
        row = 4
        flat = jnp.concatenate([ref[...] for ref in line_refs], axis=1)
        d = sums_ref.shape[1]
        for at in range(0, flat.shape[1], d):
            sums_ref[row : row + 1, :] = flat[:, at : at + d]
            row += 1

    sums_ref[0:1] += jnp.sum(da * normed, axis=0, keepdims=True)
    sums_ref[1:2] += jnp.sum(dm * normed, axis=0, keepdims=True)
    sums_ref[2:3] += jnp.sum(da, axis=0, keepdims=True)
    sums_ref[3:4] += jnp.sum(dm, axis=0, keepdims=True)


def params():
    return pltpu.CompilerParams(
        dimension_semantics=("arbitrary",), vmem_limit_bytes=VMEM
    )


def whole(shape):
    return pl.BlockSpec(shape, lambda *_: (0,) * len(shape), pipeline_mode=pl.Buffered(1))


def whole_out(shape):
    return pl.BlockSpec(shape, lambda *_: (0,) * len(shape))


def waiting(kernel, count, where):
    if not count:
        return kernel

    def body(*refs):
        kernel(*refs[:where], *refs[where + count :])

    return body


def after(x, *deps):
    def body(x_ref, *refs):
        pass

    any_spec = pl.BlockSpec(memory_space=pl.ANY)
    return pl.pallas_call(
        body,
        in_specs=[any_spec] * (1 + len(deps)),
        out_specs=any_spec,
        out_shape=jax.ShapeDtypeStruct(x.shape, x.dtype),
        input_output_aliases={0: 0},
        name="after",
    )(x, *deps)


def any_specs(deps):
    return [pl.BlockSpec(memory_space=pl.ANY)] * len(deps)


def cost(*_):
    return pl.CostEstimate(flops=1024, bytes_accessed=1024, transcendentals=0)


def scalar_in():
    return pl.BlockSpec(memory_space=pltpu.SMEM)


def run_norm(me, tokens, cotangent, gains, biases, steps, deps=()):
    rows, d = tokens.shape
    by_row = pl.BlockSpec((N_ROWS, d), lambda i: (i, 0))
    by_col = pl.BlockSpec((d, N_ROWS), lambda i: (0, i))
    flat = jax.ShapeDtypeStruct((rows, d), BF16)
    turned = jax.ShapeDtypeStruct((d, rows), BF16)
    return pl.pallas_call(
        waiting(functools.partial(norm_kernel, steps), len(deps), 5),
        grid=(rows // N_ROWS,),
        in_specs=[scalar_in(), by_row, by_row, whole((2, d)), whole((2, d))] + any_specs(deps),
        out_specs=[by_row, by_row, by_col, by_col, by_col, by_col, whole_out((1, d))],
        out_shape=[flat, flat, turned, turned, turned, turned, jax.ShapeDtypeStruct((1, d), F32)],
        compiler_params=params(),
        cost_estimate=cost(40 * rows * d, 16 * rows * d),
        name="norm",
    )(me, tokens, cotangent, gains, biases, *deps)


def run_attn(x, xt, dy, dyt, w, bqk, bv, tables, heads, deps=()):
    rows, d = x.shape
    nqk, nv = heads * PAIR, heads * HEAD_DIM
    width = nqk + 2 * nv
    chunks = w.shape[1] // width
    member = lambda t: pl.BlockSpec((d, width // heads), lambda j, t=t: (0, t * chunks + j))
    per = lambda n: pl.BlockSpec((1, n), lambda j: (0, j))
    tall = lambda n: pl.BlockSpec((rows, n), lambda j: (0, j))
    half = (heads // 2, rows, PAIR)
    return pl.pallas_call(
        waiting(functools.partial(attn_kernel, heads), len(deps), 9 + heads),
        grid=(chunks,),
        in_specs=[member(t) for t in range(heads)]
        + [
            whole((rows, d)),
            whole((d, rows)),
            whole((rows, d)),
            whole((d, rows)),
            per(nqk),
            per(nv),
        ]
        + [whole((rows, PAIR))] * 3
        + any_specs(deps),
        out_specs=[
            tall(nv),
            tall(nqk),
            tall(nv),
            pl.BlockSpec((d, width), lambda j: (0, j)),
            per(nqk),
            per(nv),
        ],
        out_shape=[
            jax.ShapeDtypeStruct((rows, chunks * nv), BF16),
            jax.ShapeDtypeStruct((rows, chunks * nqk), BF16),
            jax.ShapeDtypeStruct((rows, chunks * nv), BF16),
            jax.ShapeDtypeStruct((d, chunks * width), BF16),
            jax.ShapeDtypeStruct((1, chunks * nqk), F32),
            jax.ShapeDtypeStruct((1, chunks * nv), F32),
        ],
        scratch_shapes=[
            pltpu.VMEM((heads, rows, PAIR), BF16),
            pltpu.VMEM(half, BF16),
            pltpu.VMEM(half, BF16),
            pltpu.VMEM((2, rows, PAIR), F32),
            pltpu.VMEM((2, PAIR, rows), F32),
            pltpu.VMEM((PAIR, rows), F32),
            pltpu.VMEM((rows, PAIR), F32),
            pltpu.VMEM((2, rows, rows), F32),
            pltpu.VMEM((2, rows, rows), F32),
            pltpu.VMEM((2, rows, rows), BF16),
            pltpu.VMEM((2, rows, rows), BF16),
        ],
        compiler_params=params(),
        cost_estimate=cost(
            4 * rows * d * chunks * width + 24 * chunks * heads * rows * rows * PAIR,
            20 * rows * d,
            chunks * heads * rows * rows,
        ),
        name="attention",
    )(*[w] * heads, x, xt, dy, dyt, bqk, bv, *tables, *deps)


def run_mlp(x, xt, dy, dyt, w, b, heads, first, count, deps=()):
    rows, d = x.shape
    n = FF_CHUNK
    parts = w.shape[1] // (2 * n * heads)
    width = heads * n
    half = d // 2
    by = lambda r, dt: jax.ShapeDtypeStruct((r, count * width), dt)
    member = lambda t, k: pl.BlockSpec((d, n), lambda p: (0, (t * parts + first + p) * 2 + k))
    tall = lambda r: pl.BlockSpec((r, width), lambda p: (0, p))
    return pl.pallas_call(
        waiting(functools.partial(mlp_kernel, heads), len(deps), 5 + 2 * heads),
        grid=(count,),
        in_specs=[
            whole((rows, d)),
            whole((d, rows)),
            whole((rows, d)),
            whole((d, rows)),
            pl.BlockSpec((1, width), lambda p: (0, first + p)),
        ]
        + [member(t, k) for k in range(2) for t in range(heads)]
        + any_specs(deps),
        out_specs=[whole_out((rows, d))] * 2 + [tall(half)] * 4 + [tall(1)],
        out_shape=[jax.ShapeDtypeStruct((rows, d), BF16)] * 2 + [by(half, BF16)] * 4 + [by(1, F32)],
        scratch_shapes=[pltpu.VMEM((rows, width), BF16)] * 2 + [pltpu.VMEM((rows, d), F32)] * 2,
        compiler_params=params(),
        cost_estimate=cost(),
        name="mlp",
    )(x, xt, dy, dyt, b, *[w] * (2 * heads), *deps)


def full_spec(x):
    return pl.BlockSpec(x.shape, lambda *_: (0,) * x.ndim)


def simple_call(kernel, name, ins, outs, deps=(), scratch=(), scalars=0):
    vmem = pl.BlockSpec(memory_space=pltpu.VMEM)
    return pl.pallas_call(
        waiting(kernel, len(deps), len(ins)),
        in_specs=[scalar_in()] * scalars + [vmem] * (len(ins) - scalars) + any_specs(deps),
        out_specs=[vmem] * len(outs),
        out_shape=[jax.ShapeDtypeStruct(shape, dt) for shape, dt in outs],
        scratch_shapes=scratch,
        compiler_params=pltpu.CompilerParams(vmem_limit_bytes=VMEM),
        cost_estimate=cost(),
        name=name,
    )(*ins, *deps)


def run_fold(arrays, deps=()):
    rows, n = arrays[0].shape
    half = rows // 2
    outs = [((half, n), BF16)] * 4
    if len(arrays) > 4:
        count, d = arrays[4].shape
        outs[1] = ((half + 2 * count * -(-d // n), n), BF16)
        outs.append(((count, d), F32))
    return simple_call(fold_kernel, "fold", arrays, outs, deps)


def run_split(arrays, size, n, deps=()):
    rows, width = arrays[0].shape
    width = 2 * width // size
    lined = len(arrays) > 4
    if lined:
        count, d = arrays[4].shape
        rows += 2 * count * -(-d // width)
    outs = [((rows, width), BF16)] * size
    return simple_call(functools.partial(split_kernel, n, lined), "split", arrays, outs, deps)


def run_heads(kernel, name, acts, w, heads, groups, deps=()):
    rows, d = acts[0].shape[0], w.shape[0]
    tall = lambda n: pl.BlockSpec((M_ROWS, n), lambda i: (i, 0))
    return pl.pallas_call(
        waiting(functools.partial(kernel, groups, heads), len(deps), len(acts) + 1),
        grid=(rows // M_ROWS,),
        in_specs=[tall(u.shape[1]) for u in acts] + [whole(w.shape)] + any_specs(deps),
        out_specs=tall(d),
        out_shape=jax.ShapeDtypeStruct((rows, d), BF16),
        compiler_params=params(),
        cost_estimate=cost(),
        name=name,
    )(*acts, w, *deps)


def run_last(tokens, dy, ya, da, gains, branch_bias, ym, dm, lines, deps):
    rows, d = tokens.shape
    by_row = pl.BlockSpec((N_ROWS, d), lambda i: (i, 0))
    parts = len(ym)
    count = -(-(4 + sum(u.shape[1] for u in lines) // d) // 8) * 8
    return pl.pallas_call(
        waiting(functools.partial(last_kernel, parts, len(lines)), len(deps), 6 + 2 * parts + len(lines)),
        grid=(rows // N_ROWS,),
        in_specs=[by_row] * 4
        + [whole((2, d))] * 2
        + [by_row] * (2 * parts)
        + [whole(u.shape) for u in lines]
        + any_specs(deps),
        out_specs=[by_row, by_row, whole_out((count, d))],
        out_shape=[
            jax.ShapeDtypeStruct((rows, d), BF16),
            jax.ShapeDtypeStruct((rows, d), F32),
            jax.ShapeDtypeStruct((count, d), F32),
        ],
        compiler_params=params(),
        cost_estimate=cost(60 * rows * d, 44 * rows * d),
        name="last",
    )(tokens, dy, ya, da, gains, branch_bias, *ym, *dm, *lines, *deps)


def ring(x, size, shift):
    return lax.ppermute(x, "tensor", [(i, (i - shift) % size) for i in range(size)])


def flip(x, size, bit):
    return lax.ppermute(x, "dp", [(i, i ^ bit) for i in range(size)])


def bits_of(size):
    return [1 << b for b in range(size.bit_length() - 1)]


def rotate_parts(parts, size):
    me = lax.axis_index("tensor")
    parts = jnp.stack(parts)
    return lax.dynamic_slice_in_dim(
        jnp.concatenate([parts, parts]), lax.rem(size - me, size), size, 0
    )


def gather_dp(x, size):
    me = lax.axis_index("dp")
    x = x[None]
    for bit in bits_of(size):
        other = flip(x, size, bit)
        mine_high = (me & bit) != 0
        x = jnp.concatenate([jnp.where(mine_high, other, x), jnp.where(mine_high, x, other)])
    return x


def send_blocks(blocks, size):
    return [blocks[0]] + [ring(blocks[s], size, size - s) for s in range(1, size)]


def rope_tables():
    positions = jnp.arange(SEQ_LEN, dtype=F32)
    frequency = 10000.0 ** (-2.0 * jnp.arange(ROT // 2, dtype=F32) / ROT)
    angles = positions[:, None] * frequency[None, :]
    cosine, sine = jnp.cos(angles), jnp.sin(angles)
    none = jnp.zeros_like(sine)
    rest = jnp.zeros((SEQ_LEN, HEAD_DIM - ROT), F32)
    c = jnp.concatenate([cosine, cosine, rest + 1.0], axis=1)
    s1 = jnp.concatenate([-sine, none, rest], axis=1)
    s2 = jnp.concatenate([none, sine, rest], axis=1)
    scale = HEAD_DIM**-0.5
    return [jnp.concatenate([u * scale, u], axis=1) for u in (c, s1, s2)]


def on_device(
    dp,
    tp,
    tokens,
    ln_gains,
    ln_biases,
    w_query,
    w_key,
    w_value,
    query_bias,
    key_bias,
    value_bias,
    w_output,
    w_up,
    up_bias,
    w_down,
    out_biases,
    cotangent,
):
    rows, d = tokens.shape
    own = w_query.shape[0]
    groups = w_query.shape[1] // HEAD_DIM
    hidden = w_up.shape[1]
    parts = hidden // FF_CHUNK
    nqk, nv = tp * PAIR, tp * HEAD_DIM
    a_width = nqk + 2 * nv
    f_width = tp * FF_CHUNK

    line = groups * 2 * PAIR
    flat = lambda u: u.reshape(1, -1)
    (pack,) = simple_call(
        functools.partial(pack_kernel, groups),
        "pack",
        [w_query, w_key, w_value, w_output, ln_gains, ln_biases, out_biases]
        + [flat(jnp.concatenate([query_bias, key_bias, value_bias, up_bias]))],
        [((16 + own, line), BF16)],
        scratch=[pltpu.VMEM((16, line), F32)],
    )
    packs = [pack] + [ring(pack, tp, s) for s in range(1, tp)]
    fa = jnp.concatenate([u[16:] for u in packs], axis=1)
    wf = jnp.stack([w.reshape(own, parts, FF_CHUNK) for w in (w_up, w_down.T)], axis=2)
    wf = after(wf.reshape(own, -1), fa)
    fa = lax.all_gather(fa, "dp", axis=0, tiled=True)
    n = ln_gains.shape[1]
    small = gather_dp(rotate_parts([u[:6, :n] for u in packs], tp), dp).astype(F32)
    small = small.transpose(2, 0, 1, 3).reshape(6, d)
    gains, biases, branch_bias = small[0:2], small[2:4], small[4:6]
    vec = jnp.stack([u[6:10] for u in packs]).astype(F32).reshape(tp, -1)
    hq = groups * HEAD_DIM
    by_head = lambda k: vec[:, k * hq : (k + 1) * hq].reshape(tp, groups, HEAD_DIM).transpose(1, 0, 2)
    bqk = flat(jnp.stack([by_head(0), by_head(1)], axis=2))
    bv = flat(by_head(2))
    bu = flat(vec[:, 3 * hq : 3 * hq + hidden].reshape(tp, parts, FF_CHUNK).transpose(1, 0, 2))
    ff_parts = [wf] + [ring(wf, tp, k) for k in range(1, tp)]

    tables = rope_tables()
    me_dp = lax.axis_index("dp").astype(jnp.int32).reshape(1)
    me_tp = lax.axis_index("tensor").astype(jnp.int32).reshape(1)
    me_all = me_dp * tp + me_tp
    bits = bits_of(dp)
    steps = (bits, bits[:1] + bits[:0:-1]) if own % 16 == 0 and len(bits) == 3 else None
    attn_in, mlp_in, attn_t, dy_t, mlp_tp, dy_tp, dy_sum = run_norm(
        me_dp, tokens, cotangent, gains, biases, steps, [bqk, bv, *tables]
    )
    ff_parts[-1] = after(ff_parts[-1], attn_in)
    ready = jnp.concatenate(ff_parts, axis=1)
    ff = lax.all_gather(ready, "dp", axis=0, tiled=True)
    o, dqk, dv, ga, dbqk, dbv = run_attn(
        attn_in, attn_t, cotangent, dy_t, fa, bqk, bv, tables, tp, [ready]
    )
    early = parts - parts // 3
    dbu, ym, dm = [], [], []
    def mlp(first, count, deps):
        y_c, dm_c, uk, us, dk, ds, db = run_mlp(
            mlp_in, mlp_tp, cotangent, dy_tp, ff, bu, tp, first, count, deps
        )
        ym.append(y_c)
        dm.append(dm_c)
        dbu.append(db)
        return [uk, us, dk, ds]

    da = run_heads(heads_back_kernel, "heads_back", [dqk, dv], fa, tp, groups)

    ga = lax.psum_scatter(after(ga, ff, da), "dp", scatter_dimension=0, tiled=True)

    def heads_out(deps):
        return run_heads(heads_out_kernel, "heads_out", [o], fa, tp, groups, deps)

    def cut(u, deps):
        outs = [((tp, own, line), BF16)]
        (u,) = simple_call(cut_kernel, "cut", [me_tp, u], outs, deps, scalars=1)
        return u

    def last(ya, deps):
        lines = [dy_sum, dbqk, dbv] + dbu
        return run_last(tokens, cotangent, ya, da, gains, branch_bias, ym, dm, lines, deps)

    def finish_heads(blocks):
        total = lax.psum_scatter(blocks, "tensor", scatter_dimension=0, tiled=True)[0]
        wide, tall = ((own, groups * HEAD_DIM), F32), ((groups * HEAD_DIM, own), F32)
        kernel = functools.partial(heads_grad_kernel, 1)
        return simple_call(kernel, "heads_grad", [total], [wide, wide, wide, tall])

    if steps is None:

        def reduce(arrays, n):
            uk, us, dk, ds = arrays
            both = []
            for keep, send in ((uk, us), (dk, ds)):
                u = jnp.concatenate([keep, send], axis=0)
                u = lax.psum_scatter(u, "dp", scatter_dimension=0, tiled=True)
                both.append(u.reshape(own, -1, tp, n))
            both = jnp.concatenate(both, axis=3)
            return send_blocks([both[:, :, s].reshape(own, -1) for s in range(tp)], tp)

        head_grads = finish_heads(cut(ga, []))
        one = reduce(mlp(0, early, []), FF_CHUNK)
        two = reduce(mlp(early, parts - early, []), FF_CHUNK)
        block_out, grad_tokens, vectors = last(heads_out([]), [])
        for bit in bits_of(dp):
            vectors = vectors + flip(vectors, dp, bit)
        lines_shape = vectors.shape
        vectors = [vectors] + [ring(vectors, tp, tp - s) for s in range(1, tp)]
    else:
        def step(arrays, at, deps, n=FF_CHUNK):
            uk, us, dk, ds, *lines = arrays
            ins = [uk, flip(us, dp, steps[0][at]), dk, flip(ds, dp, steps[1][at]), *lines]
            if lines and at == 0:
                ins.append(flip(lines[0], dp, steps[0][0]))
            if at < 2:
                return run_fold(ins, deps)
            if lines:
                return run_split(ins, tp, n, deps)
            outs = [((tp, own, 2 * uk.shape[1] // tp), BF16)]
            kernel = functools.partial(split_all_kernel, n)
            return simple_call(kernel, "split_all", [me_tp, *ins], outs, deps, scalars=1)[0]

        hold = lambda arrays, *deps: [after(u, *deps) if k in (1, 3) else u for k, u in enumerate(arrays)]
        one = mlp(0, early, [da])
        ya = heads_out([dm[0]])
        one = step(one, 0, [ya])
        two = mlp(early, parts - early, [one[1]])
        block_out, grad_tokens, lines = last(ya, [dm[1]])
        lines_shape = lines.shape
        two = hold(two, lines)
        ga = cut(ga, [lines])
        one = step(one, 1, [ga])
        two = step([*two, lines], 0, [one[1]])
        one = step(one, 2, [two[1]])
        two = step(two, 1, [one])
        two = step(two, 2, [two[1]])
        head_grads = finish_heads(ga)
        one = [lax.psum_scatter(one, "tensor", scatter_dimension=0, tiled=True)[0]]
        two = vectors = send_blocks(two, tp)
    pieces = [*one, *two]

    grad_w_query, grad_w_key, grad_w_value, grad_w_output = head_grads
    grad_ln_gains, grad_ln_biases, grad_out_biases, gqb, gkb, gvb, gub = simple_call(
        functools.partial(vector_kernel, tp, groups, parts, own, *lines_shape),
        "vectors",
        [me_all] + vectors,
        [((2, n), F32)] * 3 + [((1, groups * HEAD_DIM), F32)] * 3 + [((1, hidden), F32)],
        scalars=1,
    )
    grad_w_up, grad_w_down = simple_call(
        functools.partial(mlp_grad_kernel, (len(one), len(two))),
        "mlp_grad",
        pieces,
        [((own, hidden), F32)] * 2,
    )
    return (
        block_out,
        grad_tokens,
        grad_ln_gains,
        grad_ln_biases,
        grad_w_query,
        grad_w_key,
        grad_w_value,
        gqb.reshape(-1),
        gkb.reshape(-1),
        gvb.reshape(-1),
        grad_w_output,
        grad_w_up,
        gub.reshape(-1),
        grad_w_down.T,
        grad_out_biases,
    )


def solution(mesh):
    rows = P(("dp", "tensor"), None)
    cols = P(None, ("dp", "tensor"))
    wide, tall, vec = P("dp", "tensor"), P("tensor", "dp"), P("tensor")
    return jax.shard_map(
        functools.partial(on_device, mesh.shape["dp"], mesh.shape["tensor"]),
        mesh=mesh,
        in_specs=(rows, cols, cols, wide, wide, wide, vec, vec, vec, tall, wide, vec, tall, cols, rows),
        out_specs=(
            rows, rows, cols, cols, wide, wide, wide, vec, vec, vec, tall, wide, vec, tall, cols,
        ),
        check_vma=False,
    )
```
